32 devices in a mesh: scan: 2 (over x), row: 16 (over z, y, core).
Axes of the slice: x: 2, y: 2, z: 4, core: 2. Of those that a mesh axis runs over, the one named last changes fastest.
Arguments:
- object_field: float32 [4, 2, 3072, 384], P('scan', None, 'row'), parts along dimension 0, may hold values from -2.5 to 2.5
- probe: float32 [4, 256, 256], P('scan'), parts along dimension 0, may hold values from -4 to 4
- intensity: float32 [64, 256, 256], P(('scan', 'row')), parts along dimension 0, may hold values from 0 to 3
- row_offset: int32 [64], P(('scan', 'row')), parts along dimension 0, may hold values from 0 to 64
- col_offset: int32 [64], P(('scan', 'row')), parts along dimension 0, may hold values from 0 to 128
- slice_first: int32 [64], P(('scan', 'row')), parts along dimension 0, may hold values from 0 to 1
Outputs:
- object_out: float32 [4, 2, 3072, 384], P('scan', None, 'row'), parts along dimension 0
- probe_out: float32 [4, 256, 256], P('scan'), parts along dimension 0
- misfit_mean: float32 [4], P('scan'), parts along dimension 0
The draws below stay inside these ranges and needn't reach their ends.
There are 2 independent parts, one for each index of `scan`. The reference program is written for one: setup_inputs(seed, part) draws one part's arguments, and reference() takes and returns one part's arrays. A program takes and returns all parts, laid end to end along the dimension named above; each array names one. Nothing has to cross between parts.
All inputs are finite; a program needn't handle non-finite values.
Results may differ from the reference program's by a relative error of at most 0.0003.
Values sent between devices are 32-bit elements; how exact they have to be, the bound alone decides.
A program may use at most 128 MiB of HBM per device.

```python
import jax
import jax.numpy as jnp
from jax import lax

PROBE = 256
TILE = 192
COLS = 384
MARGIN = 64
POS = 2
ITERS = 2
ROWS = 3072
POS_TOTAL = 32
N_ROW = 16


def draw_object_field(key, part):
    key = jax.random.fold_in(key, 11)
    first_key, second_key = jax.random.split(key)
    rows_scaled = jnp.arange(ROWS, dtype=jnp.float32) / ROWS
    magnitude = jax.random.uniform(first_key, (2, ROWS, COLS), jnp.float32, 0.6, 1.4)
    rising = 1.0 + 0.732 * rows_scaled
    phases = jax.random.uniform(second_key, (2, ROWS, COLS), jnp.float32, -jnp.pi, jnp.pi)
    amplitude = magnitude * rising[None, :, None]
    return jnp.stack([amplitude * jnp.cos(phases), amplitude * jnp.sin(phases)], axis=1)


def with_ends(array, stream_key, low, top_value):
    dims = array.shape
    place = [jax.random.randint(jax.random.fold_in(stream_key, axis), (), 0, dims[axis]) for axis in range(len(dims))]
    array = array.at[tuple(place)].set(low)
    longest = dims.index(max(dims))
    place[longest] = (place[longest] + 1) % dims[longest]
    return array.at[tuple(place)].set(top_value)


def steps_of(own_key, dims, cuts, least, high):
    level, own = 1.0, jax.random.fold_in(own_key, 6)
    for dim, shards_of in cuts:
        heights = jnp.exp(jax.random.uniform(jax.random.fold_in(own, dim), (shards_of,), jnp.float32, least / len(cuts), high / len(cuts)))
        level = level * jnp.repeat(heights, dims[dim] // shards_of).reshape([-1 if axis == dim else 1 for axis in range(len(dims))])
    return level


def gaussian(stream_key, shape, spread, bound, held_as=jnp.bfloat16):
    return jnp.clip(spread * jax.random.normal(stream_key, shape, jnp.float32), -bound, bound).astype(held_as)


def setup_inputs(seed: int = 0, part: int = 0) -> dict:
    key_list = jax.random.split(jax.random.key(seed), 7)
    part_keys = jax.random.split(jax.random.fold_in(key_list[6], part), 7)
    return {
        "object_field": draw_object_field(jax.random.fold_in(jax.random.fold_in(key_list[6], part), 71), part),
        "probe": gaussian(part_keys[1], (2, PROBE, PROBE), 0.7, 4.0, jnp.float32),
        "intensity": jnp.clip(3.0 * jax.random.uniform(part_keys[2], (POS_TOTAL, PROBE, PROBE), jnp.float32) ** steps_of(part_keys[2], (POS_TOTAL, PROBE, PROBE), ((0, 16),), -0.2, 0.2), 0.0, 3.0),
        "row_offset": with_ends(jax.random.randint(part_keys[3], (POS_TOTAL,), 0, TILE + 2 * MARGIN - PROBE + 1), jax.random.fold_in(part_keys[3], 1), 0, TILE + 2 * MARGIN - PROBE).astype(jnp.int32),
        "col_offset": with_ends(jax.random.randint(part_keys[4], (POS_TOTAL,), 0, COLS - PROBE + 1), jax.random.fold_in(part_keys[4], 1), 0, COLS - PROBE).astype(jnp.int32),
        "slice_first": with_ends(jax.random.randint(part_keys[5], (POS_TOTAL,), 0, 2), jax.random.fold_in(part_keys[5], 1), 0, 1).astype(jnp.int32),
    }


SMOOTHING = 0.01
OBJECT_RATE = 0.25
PROBE_RATE = 0.5
PROPAGATION = 4.0
DAMPING = 1.0
TINY = 1e-06

def propagation_kernel(length):
    counter = jnp.arange(length, dtype=jnp.int32)
    signed = jnp.where(counter < length // 2, counter, counter - length).astype(jnp.float32) / length
    phases = -jnp.pi * PROPAGATION * (signed[:, None] ** 2 + signed[None, :] ** 2)
    return lax.complex(jnp.cos(phases), jnp.sin(phases))

def local_terms(extended, probe_now, seen, rows_at, cols_at, order, kernel):
    anchor = jnp.zeros((), jnp.int32)

    def objective(extended, probe_now):
        wave_probe = lax.complex(probe_now[0], probe_now[1])
        total = jnp.zeros((), jnp.float32)
        weight = jnp.zeros((1, PROBE, PROBE), jnp.float32)
        for index in range(POS):
            patch = lax.dynamic_slice(extended, (anchor, anchor, rows_at[index], cols_at[index]), (2, 2, PROBE, PROBE))
            chosen = order[index] == 0
            front = jnp.where(chosen, patch[0], patch[1])
            behind = jnp.where(chosen, patch[1], patch[0])
            wave = wave_probe * lax.complex(front[0], front[1])
            near = jnp.fft.ifft2(jnp.fft.fft2(wave, norm='ortho') * kernel, norm='ortho')
            far_field = jnp.fft.fft2(near * lax.complex(behind[0], behind[1]), norm='ortho')
            modulus = jnp.sqrt(jnp.real(far_field) ** 2 + jnp.imag(far_field) ** 2 + SMOOTHING)
            misfit = modulus - jnp.sqrt(seen[index] + SMOOTHING)
            total = total + jnp.sum(misfit * misfit)
            weight = weight + (front[0] * front[0] + front[1] * front[1])[None]
        return (total, weight)
    total, pullback, weight = jax.vjp(objective, extended, probe_now, has_aux=True)
    grad_ext, grad_probe = pullback(jnp.ones_like(total))
    return (grad_ext, grad_probe, weight, total)

def reference(object_field, probe, intensity, row_offset, col_offset, slice_first):
    kernel = propagation_kernel(PROBE)
    extent = TILE + 2 * MARGIN
    anchor = jnp.zeros((), jnp.int32)
    field = object_field
    current = probe
    losses = []
    for step in range(ITERS):
        padded = jnp.pad(field, ((0, 0), (0, 0), (MARGIN, MARGIN), (0, 0)))

        def per_device(device, padded=padded, current=current):
            extended = lax.dynamic_slice(padded, (anchor, anchor, device * TILE, anchor), (2, 2, extent, COLS))
            first = device * POS
            seen = lax.dynamic_slice_in_dim(intensity, first, POS, 0)
            rows_at = lax.dynamic_slice_in_dim(row_offset, first, POS, 0)
            cols_at = lax.dynamic_slice_in_dim(col_offset, first, POS, 0)
            order = lax.dynamic_slice_in_dim(slice_first, first, POS, 0)
            return local_terms(extended, current, seen, rows_at, cols_at, order, kernel)
        grad_ext, grad_probe, weight, total = lax.map(per_device, jnp.arange(N_ROW, dtype=jnp.int32))
        core = grad_ext[:, :, :, MARGIN:MARGIN + TILE]
        upper = grad_ext[:, :, :, :MARGIN]
        lower = grad_ext[:, :, :, extent - MARGIN:]
        core = core.at[:-1, :, :, TILE - MARGIN:].add(upper[1:])
        core = core.at[1:, :, :, :MARGIN].add(lower[:-1])
        grad_field = jnp.transpose(core, (1, 2, 0, 3, 4)).reshape(2, 2, TILE * N_ROW, COLS)
        rate = OBJECT_RATE / (jnp.mean(current[0] * current[0] + current[1] * current[1]) + TINY)
        field = field - rate * grad_field
        current = current - PROBE_RATE * lax.optimization_barrier(jnp.sum(grad_probe, axis=0)) / (lax.optimization_barrier(jnp.sum(weight, axis=0)) + DAMPING)
        losses.append(jnp.sum(total) / (POS_TOTAL * PROBE * PROBE))
    return (field, current, jnp.stack(losses))
```

```python
import functools

import jax
import jax.numpy as jnp
import ml_dtypes
import numpy as np
from jax import lax
from jax.experimental import pallas as pl
from jax.experimental.pallas import tpu as pltpu
from jax.sharding import PartitionSpec as P

MARGIN = 64
ITERS = 2
SMOOTHING = 0.01
OBJECT_RATE = 0.25
PROBE_RATE = 0.5
PROPAGATION = 4.0
DAMPING = 1.0
TINY = 1e-06


def split_table(table):
    left = np.block([[table.real, -table.imag], [table.imag, table.real]])
    high = left.astype(ml_dtypes.bfloat16)
    low = (left - high.astype(np.float64)).astype(ml_dtypes.bfloat16)
    on_left = np.concatenate([high, low, high], axis=1)
    on_right = np.concatenate([high.T, high.T, low.T], axis=0)
    return np.ascontiguousarray(on_left), np.ascontiguousarray(on_right)


@functools.lru_cache(maxsize=None)
def tables(length):
    counter = np.arange(length)
    dft = np.exp(-2j * np.pi / length * ((counter[:, None] * counter[None, :]) % length))
    dft = dft / np.sqrt(length)
    signed = np.where(counter < length // 2, counter, counter - length) / length
    phase = np.exp(-1j * np.pi * PROPAGATION * signed**2)
    spread = (np.conj(dft) * phase[None, :]) @ dft
    return split_table(dft) + split_table(spread)


def halves(value):
    high = value.astype(jnp.bfloat16)
    low = (value - high.astype(jnp.float32)).astype(jnp.bfloat16)
    return high, low


def both_sides(re, im, on_left, on_right):
    length = re.shape[0]
    high, low = halves(jnp.concatenate([re, im], axis=1))
    rows = jnp.dot(
        jnp.concatenate([high, low, high], axis=1),
        on_right[...],
        preferred_element_type=jnp.float32,
    )
    stacked = jnp.concatenate([rows[:, :length], rows[:, length:]], axis=0)
    high, low = halves(stacked)
    done = jnp.dot(
        on_left[...],
        jnp.concatenate([high, high, low], axis=0),
        preferred_element_type=jnp.float32,
    )
    return done[:length], done[length:]


def times(a_re, a_im, b_re, b_im):
    return a_re * b_re - a_im * b_im, a_re * b_im + a_im * b_re


def local_kernel(
    rows_ref, cols_ref, first_ref, field, probe, intensity, dft_l, dft_r, spread_l, spread_r,
    grad, sums, window,
):
    length = probe.shape[1]
    width = field.shape[3]
    grad[...] = jnp.zeros_like(grad)
    sums[...] = jnp.zeros_like(sums)

    @pl.loop(0, intensity.shape[0])
    def _(index):
        row = rows_ref[index]
        col = cols_ref[index]
        base = pl.multiple_of(jnp.minimum(row // 8 * 8, field.shape[2] - length - 8), 8)
        extra = row - base
        up = lax.rem(length + 8 - extra, length + 8)
        taken = pl.ds(base, length + 8)
        chosen = first_ref[index] == 0
        back = lax.rem(width - col, width)
        for which in range(2):
            for part in range(2):
                wide = pltpu.roll(field[which, part, taken, :], back, 1)[:, :length]
                window[which, part] = pltpu.roll(wide, up, 0)[:length]
        front_at = jnp.where(chosen, 0, 1)
        behind_at = 1 - front_at
        front_re, front_im = window[front_at, 0], window[front_at, 1]
        wave_re, wave_im = times(probe[0], probe[1], front_re, front_im)
        sums[2 * length : 3 * length] += front_re * front_re + front_im * front_im
        near_re, near_im = both_sides(wave_re, wave_im, spread_l, spread_r)
        exit_re, exit_im = times(near_re, near_im, window[behind_at, 0], window[behind_at, 1])
        far_re, far_im = both_sides(exit_re, exit_im, dft_l, dft_r)
        modulus = jnp.sqrt(far_re * far_re + far_im * far_im + SMOOTHING)
        misfit = modulus - jnp.sqrt(intensity[index] + SMOOTHING)
        squares = (misfit * misfit).reshape(length // 8, 8, length)
        sums[3 * length : 3 * length + 8] += jnp.sum(squares, axis=0)
        slope = 2.0 * misfit / modulus
        exit_re, exit_im = both_sides(slope * far_re, -slope * far_im, dft_l, dft_r)
        behind_re, behind_im = times(near_re, near_im, exit_re, exit_im)
        near_re, near_im = times(window[behind_at, 0], window[behind_at, 1], exit_re, exit_im)
        wave_re, wave_im = both_sides(near_re, near_im, spread_l, spread_r)
        probe_re, probe_im = times(window[front_at, 0], window[front_at, 1], wave_re, wave_im)
        sums[:length] += probe_re
        sums[length : 2 * length] -= probe_im
        front_re, front_im = times(probe[0], probe[1], wave_re, wave_im)
        below = jnp.zeros((8, length), jnp.float32)
        beside = jnp.zeros((length + 8, width - length), jnp.float32)
        for which, part, value in (
            (front_at, 0, front_re),
            (front_at, 1, -front_im),
            (behind_at, 0, behind_re),
            (behind_at, 1, -behind_im),
        ):
            value = pltpu.roll(jnp.concatenate([value, below], axis=0), extra, 0)
            wide = pltpu.roll(jnp.concatenate([value, beside], axis=1), col, 1)
            grad[which, part, taken, :] += wide


def local_terms(field, probe, intensity, rows, cols, first):
    length = probe.shape[1]
    vmem = pl.BlockSpec(memory_space=pltpu.VMEM)
    smem = pl.BlockSpec(memory_space=pltpu.SMEM)
    return pl.pallas_call(
        local_kernel,
        out_shape=(
            jax.ShapeDtypeStruct(field.shape, jnp.float32),
            jax.ShapeDtypeStruct((3 * length + 8, length), jnp.float32),
        ),
        in_specs=[smem] * 3 + [vmem] * 7,
        out_specs=(vmem, vmem),
        scratch_shapes=[pltpu.VMEM((2, 2, length, length), jnp.float32)],
        compiler_params=pltpu.CompilerParams(vmem_limit_bytes=48 * 1024 * 1024),
    )(rows, cols, first, field, probe, intensity, *(jnp.asarray(t) for t in tables(length)))


def from_sides(to_before, to_after):
    devices = lax.axis_size("row")
    up = [(i, i + 1) for i in range(devices - 1)]
    down = [(i + 1, i) for i in range(devices - 1)]
    return lax.ppermute(to_after, "row", up), lax.ppermute(to_before, "row", down)


def shards(object_field, probe, intensity, row_offset, col_offset, slice_first):
    length = probe.shape[1]
    tile = object_field.shape[2]
    count = intensity.shape[0] * lax.axis_size("row") * length * length
    before, after = from_sides(object_field[:, :, :MARGIN], object_field[:, :, tile - MARGIN :])
    field = jnp.concatenate([before, object_field, after], axis=2)
    here = lax.axis_index("row")
    inside = jnp.arange(tile + 2 * MARGIN)[:, None]
    inside = ((inside >= MARGIN) | (here > 0)) & (
        (inside < tile + MARGIN) | (here < lax.axis_size("row") - 1)
    )
    losses = []
    for step in range(ITERS):
        grad, sums = local_terms(field, probe, intensity, row_offset, col_offset, slice_first)
        rate = OBJECT_RATE / (jnp.mean(probe[0] * probe[0] + probe[1] * probe[1]) + TINY)
        sums = lax.psum(sums, "row")
        if step < ITERS - 1:
            before, after = from_sides(grad[:, :, : 2 * MARGIN], grad[:, :, tile:])
            middle = jnp.zeros_like(grad[:, :, : tile - 2 * MARGIN])
            grad = grad + jnp.concatenate([before, middle, after], axis=2)
            field = jnp.where(inside, field - rate * grad, 0.0)
        else:
            before, after = from_sides(grad[:, :, :MARGIN], grad[:, :, tile + MARGIN :])
            middle = jnp.zeros_like(grad[:, :, : tile - 2 * MARGIN])
            grad = grad[:, :, MARGIN : tile + MARGIN] + jnp.concatenate(
                [before, middle, after], axis=2
            )
            field = field[:, :, MARGIN : tile + MARGIN] - rate * grad
        summed = sums[: 2 * length].reshape(2, length, length)
        weight = sums[2 * length : 3 * length]
        probe = probe - PROBE_RATE * summed / (weight + DAMPING)
        losses.append(jnp.sum(sums[3 * length :]) / count)
    return field, probe, jnp.stack(losses)


def solution(mesh):
    placed = (
        P("scan", None, "row", None),
        P("scan", None, None),
        P(("scan", "row"), None, None),
        P(("scan", "row")),
        P(("scan", "row")),
        P(("scan", "row")),
    )
    return jax.shard_map(
        shards,
        mesh=mesh,
        in_specs=placed,
        out_specs=(P("scan", None, "row", None), P("scan", None, None), P("scan")),
        check_vma=False,
    )
```

```python
import functools

import jax
import jax.numpy as jnp
import ml_dtypes
import numpy as np
from jax import lax
from jax.experimental import pallas as pl
from jax.experimental.pallas import tpu as pltpu
from jax.sharding import PartitionSpec as P

MARGIN = 64
ITERS = 2
SMOOTHING = 0.01
OBJECT_RATE = 0.25
PROBE_RATE = 0.5
PROPAGATION = 4.0
DAMPING = 1.0
TINY = 1e-06
LANES = 128
VMEM_LIMIT = 48 * 1024 * 1024
MESH = pl.DeviceIdType.MESH


def split_table(table):
    left = np.block([[table.real, -table.imag], [table.imag, table.real]])
    high = left.astype(ml_dtypes.bfloat16)
    low = (left - high.astype(np.float64)).astype(ml_dtypes.bfloat16)
    on_left = np.concatenate([high, low, high], axis=1)
    on_right = np.concatenate([high.T, high.T, low.T], axis=0)
    return np.ascontiguousarray(on_left), np.ascontiguousarray(on_right)


@functools.lru_cache(maxsize=None)
def tables(length):
    counter = np.arange(length)
    dft = np.exp(-2j * np.pi / length * ((counter[:, None] * counter[None, :]) % length))
    dft = dft / np.sqrt(length)
    signed = np.where(counter < length // 2, counter, counter - length) / length
    phase = np.exp(-1j * np.pi * PROPAGATION * signed**2)
    spread = (np.conj(dft) * phase[None, :]) @ dft
    return split_table(dft) + split_table(spread)


def halves(value):
    high = value.astype(jnp.bfloat16)
    low = (value - high.astype(jnp.float32)).astype(jnp.bfloat16)
    return high, low


def both_sides(re, im, on_left, on_right):
    length = re.shape[0]
    high, low = halves(jnp.concatenate([re, im], axis=1))
    rows = jnp.dot(
        jnp.concatenate([high, low, high], axis=1),
        on_right[...],
        preferred_element_type=jnp.float32,
    )
    stacked = jnp.concatenate([rows[:, :length], rows[:, length:]], axis=0)
    high, low = halves(stacked)
    done = jnp.dot(
        on_left[...],
        jnp.concatenate([high, high, low], axis=0),
        preferred_element_type=jnp.float32,
    )
    return done[:length], done[length:]


def times(a_re, a_im, b_re, b_im):
    return a_re * b_re - a_im * b_im, a_re * b_im + a_im * b_re


def joined(ref, plane, length):
    rows = ref.shape[1]
    return jnp.concatenate(
        [ref[plane, start : start + length] for start in range(0, rows, length)], axis=1
    )


def local_kernel(
    rows_ref, cols_ref, first_ref, field, probe, intensity, dft_l, dft_r, spread_l, spread_r,
    grad, sums, loss, window,
):
    length = intensity.shape[1]
    width = field.shape[3]
    grad[...] = jnp.zeros_like(grad)
    sums[...] = jnp.zeros_like(sums)
    loss[...] = jnp.zeros_like(loss)
    light_re, light_im = joined(probe, 0, length), joined(probe, 1, length)

    def collect(plane, value):
        for part in range(length // LANES):
            rows = pl.ds(part * length, length)
            sums[plane, rows, :] += value[:, part * LANES : (part + 1) * LANES]

    @pl.loop(0, intensity.shape[0])
    def _(index):
        row = rows_ref[index]
        col = cols_ref[index]
        base = pl.multiple_of(jnp.minimum(row // 8 * 8, field.shape[2] - length - 8), 8)
        extra = row - base
        up = lax.rem(length + 8 - extra, length + 8)
        taken = pl.ds(base, length + 8)
        chosen = first_ref[index] == 0
        back = lax.rem(width - col, width)
        for which in range(2):
            for part in range(2):
                wide = pltpu.roll(field[which, part, taken, :], back, 1)[:, :length]
                window[which, part] = pltpu.roll(wide, up, 0)[:length]
        front_at = jnp.where(chosen, 0, 1)
        behind_at = 1 - front_at
        front_re, front_im = window[front_at, 0], window[front_at, 1]
        wave_re, wave_im = times(light_re, light_im, front_re, front_im)
        collect(2, front_re * front_re + front_im * front_im)
        near_re, near_im = both_sides(wave_re, wave_im, spread_l, spread_r)
        exit_re, exit_im = times(near_re, near_im, window[behind_at, 0], window[behind_at, 1])
        far_re, far_im = both_sides(exit_re, exit_im, dft_l, dft_r)
        modulus = jnp.sqrt(far_re * far_re + far_im * far_im + SMOOTHING)
        misfit = modulus - jnp.sqrt(intensity[index] + SMOOTHING)
        squares = jnp.sum((misfit * misfit).reshape(length // 8, 8, length), axis=0)
        for part in range(length // LANES):
            loss[...] += squares[:, part * LANES : (part + 1) * LANES]
        slope = 2.0 * misfit / modulus
        exit_re, exit_im = both_sides(slope * far_re, -slope * far_im, dft_l, dft_r)
        behind_re, behind_im = times(near_re, near_im, exit_re, exit_im)
        near_re, near_im = times(window[behind_at, 0], window[behind_at, 1], exit_re, exit_im)
        wave_re, wave_im = both_sides(near_re, near_im, spread_l, spread_r)
        probe_re, probe_im = times(window[front_at, 0], window[front_at, 1], wave_re, wave_im)
        collect(0, probe_re)
        collect(1, -probe_im)
        front_re, front_im = times(light_re, light_im, wave_re, wave_im)
        below = jnp.zeros((8, length), jnp.float32)
        beside = jnp.zeros((length + 8, width - length), jnp.float32)
        for which, part, value in (
            (front_at, 0, front_re),
            (front_at, 1, -front_im),
            (behind_at, 0, behind_re),
            (behind_at, 1, -behind_im),
        ):
            value = pltpu.roll(jnp.concatenate([value, below], axis=0), extra, 0)
            wide = pltpu.roll(jnp.concatenate([value, beside], axis=1), col, 1)
            grad[which, part, taken, :] += wide


def local_terms(field, probe, intensity, rows, cols, first):
    length = intensity.shape[1]
    vmem = pl.BlockSpec(memory_space=pltpu.VMEM)
    smem = pl.BlockSpec(memory_space=pltpu.SMEM)
    return pl.pallas_call(
        local_kernel,
        out_shape=(
            jax.ShapeDtypeStruct(field.shape, jnp.float32),
            jax.ShapeDtypeStruct((3, length * length // LANES, LANES), jnp.float32),
            jax.ShapeDtypeStruct((8, LANES), jnp.float32),
        ),
        in_specs=[smem] * 3 + [vmem] * 7,
        out_specs=(vmem,) * 3,
        scratch_shapes=[pltpu.VMEM((2, 2, length, length), jnp.float32)],
        compiler_params=pltpu.CompilerParams(vmem_limit_bytes=VMEM_LIMIT),
    )(rows, cols, first, field, probe, intensity, *(jnp.asarray(t) for t in tables(length)))


def greet(devices):
    barrier = pltpu.get_barrier_semaphore()
    for condition, device in devices:

        @pl.when(condition)
        def _(device=device):
            pl.semaphore_signal(barrier, inc=1, device_id={"row": device}, device_id_type=MESH)

    pl.semaphore_wait(barrier, sum(condition.astype(jnp.int32) for condition, _ in devices))


def send(source, target, send_sem, recv_sem, device):
    return pltpu.make_async_remote_copy(
        src_ref=source,
        dst_ref=target,
        send_sem=send_sem,
        recv_sem=recv_sem,
        device_id={"row": device},
        device_id_type=MESH,
    )


def first_kernel(devices, own, field, above, below, send_sem, recv_sem):
    me = lax.axis_index("row")
    tile = own.shape[2]
    has_before, has_after = me > 0, me < devices - 1
    greet(((has_before, me - 1), (has_after, me + 1)))
    up = send(own.at[:, :, pl.ds(0, MARGIN)], below, send_sem.at[0], recv_sem.at[0], me - 1)
    down = send(
        own.at[:, :, pl.ds(tile - MARGIN, MARGIN)], above, send_sem.at[1], recv_sem.at[1], me + 1
    )
    pl.when(has_before)(up.start)
    pl.when(has_after)(down.start)
    field[:, :, MARGIN : MARGIN + tile] = own[...]

    @pl.when(has_before)
    def _():
        down.wait_recv()
        field[:, :, :MARGIN] = above[...]

    @pl.when(me == 0)
    def _():
        field[:, :, :MARGIN] = jnp.zeros_like(above)

    @pl.when(has_after)
    def _():
        up.wait_recv()
        field[:, :, MARGIN + tile :] = below[...]

    @pl.when(me == devices - 1)
    def _():
        field[:, :, MARGIN + tile :] = jnp.zeros_like(below)

    pl.when(has_before)(up.wait_send)
    pl.when(has_after)(down.wait_send)


def first_field(own):
    planes, parts, tile, width = own.shape
    vmem = pl.BlockSpec(memory_space=pltpu.VMEM)
    edge = pltpu.VMEM((planes, parts, MARGIN, width), jnp.float32)
    return pl.pallas_call(
        functools.partial(first_kernel, lax.axis_size("row")),
        out_shape=jax.ShapeDtypeStruct((planes, parts, tile + 2 * MARGIN, width), jnp.float32),
        in_specs=[vmem],
        out_specs=vmem,
        scratch_shapes=[edge, edge, pltpu.SemaphoreType.DMA((2,)), pltpu.SemaphoreType.DMA((2,))],
        compiler_params=pltpu.CompilerParams(
            collective_id=0, has_side_effects=True, vmem_limit_bytes=VMEM_LIMIT
        ),
    )(own)


def renew_kernel(
    devices, last, grad, sums, loss, field, probe, field_out, probe_out, loss_out,
    from_pair, loss_pair, to_peer, from_peer, renewed, above, below,
    pair_send, pair_recv, loss_sem, peer_send, peer_recv, spread_send, spread_recv,
    back_send, back_recv, edge_send, edge_recv,
):
    me = lax.axis_index("row")
    peers = devices // 2
    core, place = lax.rem(me, 2), lax.div(me, 2)
    partner = me + 1 - 2 * core
    piece = sums.shape[1] // devices
    extent, tile = field.shape[2], field.shape[2] - 2 * MARGIN
    reach = above.shape[2]
    has_before, has_after = me > 0, me < devices - 1

    def rows_of(side, index):
        return pl.ds(pl.multiple_of((side * peers + index) * piece, piece), piece)

    def to_pair(index, side):
        return send(
            sums.at[:, rows_of(side, index)], from_pair.at[index],
            pair_send.at[index], pair_recv.at[index], partner,
        )

    def to_place(index, slot):
        return send(
            to_peer.at[index], from_peer.at[slot],
            peer_send.at[index], peer_recv.at[slot], 2 * index + core,
        )

    def spread(index, slot):
        part = renewed.at[:, rows_of(core, slot)]
        return send(part, part, spread_send.at[index], spread_recv.at[slot], 2 * index + core)

    def back(index, side):
        part = renewed.at[:, rows_of(side, index)]
        return send(part, part, back_send.at[index], back_recv.at[index], partner)

    def after_me(step):
        return lax.rem(place + 1 + step, peers)

    def before_me(step):
        return lax.rem(place + peers - 1 - step, peers)

    other = me - 1 + 2 * core
    barrier = pltpu.get_barrier_semaphore()

    def signal(device):
        pl.semaphore_signal(barrier, inc=1, device_id={"row": device}, device_id_type=MESH)

    signal(partner)

    @pl.loop(0, peers - 1)
    def _(step):
        signal(2 * after_me(step) + core)

    beside = (other >= 0) & (other < devices)

    @pl.when(beside)
    def _():
        signal(other)

    pl.semaphore_wait(barrier, peers + beside.astype(jnp.int32))

    to_loss = send(loss, loss_pair, loss_sem.at[0], loss_sem.at[1], partner)
    to_loss.start()

    @pl.loop(0, peers)
    def _(step):
        to_pair(after_me(step), 1 - core).start()

    up = send(grad.at[:, :, pl.ds(0, reach)], below, edge_send.at[0], edge_recv.at[0], me - 1)
    down = send(
        grad.at[:, :, pl.ds(extent - reach, reach)], above, edge_send.at[1], edge_recv.at[1], me + 1
    )
    pl.when(has_before)(up.start)
    pl.when(has_after)(down.start)

    to_loss.wait()
    pair_loss = loss[...] + loss_pair[...]

    def add_pair(index):
        to_pair(index, core).wait_recv()
        both = sums[:, rows_of(core, index), :] + from_pair[index]
        return both

    @pl.loop(0, peers - 1)
    def _(step):
        index = after_me(step)
        both = add_pair(index)
        for plane in range(3):
            to_peer[index, plane * piece : (plane + 1) * piece] = both[plane]
        to_peer[index, 3 * piece :] = pair_loss
        to_place(index, place).start()

    both = add_pair(place)
    for plane in range(3):
        from_peer[place, plane * piece : (plane + 1) * piece] = both[plane]
    from_peer[place, 3 * piece :] = pair_loss

    square = probe[0] * probe[0] + probe[1] * probe[1]
    rate = OBJECT_RATE / (jnp.sum(square, keepdims=True) / (square.size) + TINY)

    @pl.loop(0, peers - 1)
    def _(step):
        index = before_me(step)
        to_place(index, index).wait_recv()

    total = from_peer[0]
    for index in range(1, peers):
        total = total + from_peer[index]
    loss_out[...] = total[3 * piece :]
    mine = rows_of(core, place)
    weight = total[2 * piece : 3 * piece] + DAMPING
    for part in range(2):
        step = PROBE_RATE * total[part * piece : (part + 1) * piece] / weight
        renewed[part, mine, :] = probe[part, mine, :] - step

    @pl.loop(0, peers - 1)
    def _(step):
        spread(after_me(step), place).start()

    back(place, core).start()

    first_row = MARGIN if last else 0
    planes = [(which, part) for which in range(grad.shape[0]) for part in range(grad.shape[1])]
    for which, part in planes:
        low, high = reach + first_row, extent - reach - first_row
        field_out[which, part, reach : high - first_row] = (
            field[which, part, low:high] - rate * grad[which, part, low:high]
        )

    @pl.loop(0, peers - 1)
    def _(step):
        index = before_me(step)
        spread(index, index).wait_recv()
        back(index, core).start()

    @pl.when(has_before)
    def _():
        down.wait_recv()

    @pl.when(me == 0)
    def _():
        above[...] = jnp.zeros_like(above)

    for which, part in planes:
        rows = slice(first_row, first_row + reach)
        field_out[which, part, :reach] = field[which, part, rows] - rate * (
            grad[which, part, rows] + above[which, part]
        )

    @pl.when(has_after)
    def _():
        up.wait_recv()

    @pl.when(me == devices - 1)
    def _():
        below[...] = jnp.zeros_like(below)

    for which, part in planes:
        rows = slice(extent - first_row - reach, extent - first_row)
        field_out[which, part, extent - 2 * first_row - reach :] = field[which, part, rows] - rate * (
            grad[which, part, rows] + below[which, part]
        )

    if not last:

        @pl.when(me == 0)
        def _():
            field_out[:, :, :MARGIN] = jnp.zeros(field[:, :, :MARGIN].shape, jnp.float32)

        @pl.when(me == devices - 1)
        def _():
            field_out[:, :, extent - MARGIN :] = jnp.zeros(field[:, :, :MARGIN].shape, jnp.float32)

    @pl.loop(0, peers)
    def _(index):
        back(index, 1 - core).wait_recv()

    probe_out[...] = renewed[...]

    @pl.loop(0, peers)
    def _(index):
        to_pair(index, 1 - core).wait_send()
        back(index, core).wait_send()

    @pl.loop(0, peers - 1)
    def _(step):
        index = after_me(step)
        to_place(index, place).wait_send()
        spread(index, place).wait_send()

    pl.when(has_before)(up.wait_send)
    pl.when(has_after)(down.wait_send)


def renew(grad, sums, loss, field, probe, last):
    devices = lax.axis_size("row")
    peers = devices // 2
    planes, parts, extent, width = field.shape
    piece = sums.shape[1] // devices
    reach = MARGIN if last else 2 * MARGIN
    height = extent - 2 * MARGIN if last else extent
    vmem = pl.BlockSpec(memory_space=pltpu.VMEM)
    edge = pltpu.VMEM((planes, parts, reach, width), jnp.float32)
    packet = pltpu.VMEM((peers, 3 * piece + 8, LANES), jnp.float32)
    each = pltpu.SemaphoreType.DMA((peers,))
    two = pltpu.SemaphoreType.DMA((2,))
    return pl.pallas_call(
        functools.partial(renew_kernel, devices, last),
        out_shape=(
            jax.ShapeDtypeStruct((planes, parts, height, width), jnp.float32),
            jax.ShapeDtypeStruct(probe.shape, jnp.float32),
            jax.ShapeDtypeStruct(loss.shape, jnp.float32),
        ),
        in_specs=[vmem] * 5,
        out_specs=(vmem,) * 3,
        scratch_shapes=[
            pltpu.VMEM((peers, 3, piece, LANES), jnp.float32),
            pltpu.VMEM(loss.shape, jnp.float32),
            packet,
            packet,
            pltpu.VMEM(probe.shape, jnp.float32),
            edge,
            edge,
            each, each, two, each, each, each, each, each, each, two, two,
        ],
        compiler_params=pltpu.CompilerParams(
            collective_id=2 if last else 1, has_side_effects=True, vmem_limit_bytes=VMEM_LIMIT
        ),
    )(grad, sums, loss, field, probe)


def shards(object_field, probe, intensity, row_offset, col_offset, slice_first):
    length = probe.shape[1]
    parts = length // LANES
    count = intensity.shape[0] * lax.axis_size("row") * length * length
    light = probe.reshape(2, length, parts, LANES).transpose(0, 2, 1, 3)
    light = light.reshape(2, parts * length, LANES)
    field = first_field(object_field)
    losses = []
    for step in range(ITERS):
        grad, sums, loss = local_terms(
            field, light, intensity, row_offset, col_offset, slice_first
        )
        field, light, loss = renew(grad, sums, loss, field, light, step == ITERS - 1)
        losses.append(jnp.sum(loss) / count)
    light = light.reshape(2, parts, length, LANES).transpose(0, 2, 1, 3)
    return field, light.reshape(probe.shape), jnp.stack(losses)


def solution(mesh):
    placed = (
        P("scan", None, "row", None),
        P("scan", None, None),
        P(("scan", "row"), None, None),
        P(("scan", "row")),
        P(("scan", "row")),
        P(("scan", "row")),
    )
    return jax.shard_map(
        shards,
        mesh=mesh,
        in_specs=placed,
        out_specs=(P("scan", None, "row", None), P("scan", None, None), P("scan")),
        check_vma=False,
    )
```

```python
import functools

import jax
import jax.numpy as jnp
import ml_dtypes
import numpy as np
from jax import lax
from jax.experimental import pallas as pl
from jax.experimental.pallas import tpu as pltpu
from jax.sharding import PartitionSpec as P

MARGIN = 64
ITERS = 2
SMOOTHING = 0.01
OBJECT_RATE = 0.25
PROBE_RATE = 0.5
PROPAGATION = 4.0
DAMPING = 1.0
TINY = 1e-06
LANES = 128
STRIP = 32
VMEM_LIMIT = 48 * 1024 * 1024
MESH = pl.DeviceIdType.MESH


def split_table(table):
    left = np.block([[table.real, -table.imag], [table.imag, table.real]])
    high = left.astype(ml_dtypes.bfloat16)
    low = (left - high.astype(np.float64)).astype(ml_dtypes.bfloat16)
    on_left = np.concatenate([high, low, high], axis=1)
    on_right = np.concatenate([high.T, high.T, low.T], axis=0)
    return np.ascontiguousarray(on_left), np.ascontiguousarray(on_right)


@functools.lru_cache(maxsize=None)
def tables(length):
    counter = np.arange(length)
    dft = np.exp(-2j * np.pi / length * ((counter[:, None] * counter[None, :]) % length))
    dft = dft / np.sqrt(length)
    signed = np.where(counter < length // 2, counter, counter - length) / length
    phase = np.exp(-1j * np.pi * PROPAGATION * signed**2)
    spread = (np.conj(dft) * phase[None, :]) @ dft
    return split_table(dft) + split_table(spread)


def joined(ref, plane, rows, length):
    return jnp.concatenate(
        [ref[plane, start + rows.start : start + rows.stop] for start in range(0, ref.shape[1], length)],
        axis=1,
    )


def times(a_re, a_im, b_re, b_im):
    return a_re * b_re - a_im * b_im, a_re * b_im + a_im * b_re


def local_kernel(
    rows_ref, cols_ref, first_ref, field, probe, intensity, dft_l, dft_r, spread_l, spread_r,
    grad, sums, loss, window, on_left, on_right, between, after, near,
):
    count, length = intensity.shape[:2]
    tiles = field.shape[2]
    strips = [slice(start, start + STRIP) for start in range(0, length, STRIP)]
    lane = lax.broadcasted_iota(jnp.int32, (STRIP, LANES), 1)
    row_at = [rows_ref[index] for index in range(count)]
    col_at = [cols_ref[index] for index in range(count)]
    front_at = [first_ref[index] for index in range(count)]

    def columns(index):
        return slice(index * length, (index + 1) * length)

    def set_left(index, rows, re, im):
        at = slice(index * length + rows.start, index * length + rows.stop)
        for value, start in ((re, 0), (im, length)):
            high = value.astype(jnp.bfloat16)
            low = (value - high.astype(jnp.float32)).astype(jnp.bfloat16)
            on_left[at, start : start + length] = high
            on_left[at, start + 2 * length : start + 3 * length] = low
            on_left[at, start + 4 * length : start + 5 * length] = high

    def both_sides(table_l, table_r):
        between[...] = jnp.dot(on_left[...], table_r[...], preferred_element_type=jnp.float32)
        for index in range(count):
            for rows in strips:
                at = slice(index * length + rows.start, index * length + rows.stop)
                for start in (0, length):
                    value = between[at, start : start + length]
                    high = value.astype(jnp.bfloat16)
                    low = (value - high.astype(jnp.float32)).astype(jnp.bfloat16)
                    for base, piece in ((0, high), (2 * length, high), (4 * length, low)):
                        first = base + start + rows.start
                        on_right[first : first + STRIP, columns(index)] = piece
        after[...] = jnp.dot(table_l[...], on_right[...], preferred_element_type=jnp.float32)

    def result(index, rows):
        below = slice(length + rows.start, length + rows.stop)
        return after[rows, columns(index)], after[below, columns(index)]

    grad[...] = jnp.zeros_like(grad)
    for index in range(count):
        back = lax.rem(LANES - col_at[index], LANES)
        stays = lane < LANES - col_at[index]
        for rows in strips:
            taken = pl.ds(row_at[index] + rows.start, STRIP)
            for which, source in ((0, front_at[index]), (1, 1 - front_at[index])):
                for part in range(2):
                    rolled = [
                        pltpu.roll(field[source, part, tile, taken, :], back, 1)
                        for tile in range(tiles)
                    ]
                    for tile in range(tiles - 1):
                        window[index, which, part, rows, tile * LANES : (tile + 1) * LANES] = (
                            jnp.where(stays, rolled[tile], rolled[tile + 1])
                        )
            front_re, front_im = window[index, 0, 0, rows], window[index, 0, 1, rows]
            light_re, light_im = joined(probe, 0, rows, length), joined(probe, 1, rows, length)
            set_left(index, rows, *times(light_re, light_im, front_re, front_im))

    both_sides(spread_l, spread_r)
    for index in range(count):
        for rows in strips:
            near_re, near_im = result(index, rows)
            near[index, 0, rows] = near_re
            near[index, 1, rows] = near_im
            behind_re, behind_im = window[index, 1, 0, rows], window[index, 1, 1, rows]
            set_left(index, rows, *times(near_re, near_im, behind_re, behind_im))

    both_sides(dft_l, dft_r)
    total = jnp.zeros((8, length), jnp.float32)
    for index in range(count):
        for rows in strips:
            far_re, far_im = result(index, rows)
            power = far_re * far_re + far_im * far_im + SMOOTHING
            modulus = jnp.sqrt(power)
            misfit = modulus - jnp.sqrt(intensity[index, rows] + SMOOTHING)
            total += jnp.sum((misfit * misfit).reshape(STRIP // 8, 8, length), axis=0)
            slope = 2.0 * misfit / modulus
            set_left(index, rows, slope * far_re, -slope * far_im)
    loss[...] = sum(
        total[:, start : start + LANES] for start in range(0, length, LANES)
    )

    def scatter(index, rows, source, part, value):
        col = lax.rem(col_at[index], LANES)
        moved = lane < col_at[index]
        taken = pl.ds(row_at[index] + rows.start, STRIP)
        rolled = [
            pltpu.roll(value[:, tile * LANES : (tile + 1) * LANES], col, 1)
            for tile in range(tiles - 1)
        ]
        zero = jnp.zeros_like(rolled[0])
        for tile in range(tiles):
            here = rolled[tile] if tile < tiles - 1 else zero
            ahead = rolled[tile - 1] if tile else zero
            grad[source, part, tile, taken, :] += jnp.where(moved, ahead, here)

    both_sides(dft_l, dft_r)
    for index in range(count):
        for rows in strips:
            exit_re, exit_im = result(index, rows)
            behind_re, behind_im = window[index, 1, 0, rows], window[index, 1, 1, rows]
            set_left(index, rows, *times(behind_re, behind_im, exit_re, exit_im))
            grad_re, grad_im = times(near[index, 0, rows], near[index, 1, rows], exit_re, exit_im)
            scatter(index, rows, 1 - front_at[index], 0, grad_re)
            scatter(index, rows, 1 - front_at[index], 1, -grad_im)

    both_sides(spread_l, spread_r)
    for rows in strips:
        light_re, light_im = joined(probe, 0, rows, length), joined(probe, 1, rows, length)
        planes = [jnp.zeros((STRIP, length), jnp.float32)] * 3
        for index in range(count):
            wave_re, wave_im = result(index, rows)
            front_re, front_im = window[index, 0, 0, rows], window[index, 0, 1, rows]
            probe_re, probe_im = times(front_re, front_im, wave_re, wave_im)
            planes[0] += probe_re
            planes[1] -= probe_im
            planes[2] += front_re * front_re + front_im * front_im
            grad_re, grad_im = times(light_re, light_im, wave_re, wave_im)
            scatter(index, rows, front_at[index], 0, grad_re)
            scatter(index, rows, front_at[index], 1, -grad_im)
        for plane, value in enumerate(planes):
            for part in range(length // LANES):
                at = slice(part * length + rows.start, part * length + rows.stop)
                sums[plane, at] = value[:, part * LANES : (part + 1) * LANES]


def local_terms(field, probe, intensity, rows, cols, first):
    count, length = intensity.shape[:2]
    vmem = pl.BlockSpec(memory_space=pltpu.VMEM)
    smem = pl.BlockSpec(memory_space=pltpu.SMEM)
    return pl.pallas_call(
        local_kernel,
        out_shape=(
            jax.ShapeDtypeStruct(field.shape, jnp.float32),
            jax.ShapeDtypeStruct((3, length * length // LANES, LANES), jnp.float32),
            jax.ShapeDtypeStruct((8, LANES), jnp.float32),
        ),
        in_specs=[smem] * 3 + [vmem] * 7,
        out_specs=(vmem,) * 3,
        scratch_shapes=[
            pltpu.VMEM((count, 2, 2, length, length), jnp.float32),
            pltpu.VMEM((count * length, 6 * length), jnp.bfloat16),
            pltpu.VMEM((6 * length, count * length), jnp.bfloat16),
            pltpu.VMEM((count * length, 2 * length), jnp.float32),
            pltpu.VMEM((2 * length, count * length), jnp.float32),
            pltpu.VMEM((count, 2, length, length), jnp.float32),
        ],
        compiler_params=pltpu.CompilerParams(vmem_limit_bytes=VMEM_LIMIT),
    )(rows, cols, first, field, probe, intensity, *(jnp.asarray(t) for t in tables(length)))


def greet(devices):
    barrier = pltpu.get_barrier_semaphore()
    for condition, device in devices:

        @pl.when(condition)
        def _(device=device):
            pl.semaphore_signal(barrier, inc=1, device_id={"row": device}, device_id_type=MESH)

    pl.semaphore_wait(barrier, sum(condition.astype(jnp.int32) for condition, _ in devices))


def send(source, target, send_sem, recv_sem, device):
    return pltpu.make_async_remote_copy(
        src_ref=source,
        dst_ref=target,
        send_sem=send_sem,
        recv_sem=recv_sem,
        device_id={"row": device},
        device_id_type=MESH,
    )


def first_kernel(devices, own, field, above, below, send_sem, recv_sem):
    me = lax.axis_index("row")
    tile = own.shape[2]
    has_before, has_after = me > 0, me < devices - 1
    greet(((has_before, me - 1), (has_after, me + 1)))
    up = send(own.at[:, :, pl.ds(0, MARGIN)], below, send_sem.at[0], recv_sem.at[0], me - 1)
    down = send(
        own.at[:, :, pl.ds(tile - MARGIN, MARGIN)], above, send_sem.at[1], recv_sem.at[1], me + 1
    )
    pl.when(has_before)(up.start)
    pl.when(has_after)(down.start)

    def place(start, rows, source):
        for index in range(field.shape[2]):
            columns = slice(index * LANES, (index + 1) * LANES)
            field[:, :, index, start : start + rows] = (
                jnp.zeros((2, 2, rows, LANES), jnp.float32)
                if source is None
                else source[:, :, :, columns]
            )

    place(MARGIN, tile, own)

    @pl.when(has_before)
    def _():
        down.wait_recv()
        place(0, MARGIN, above)

    @pl.when(me == 0)
    def _():
        place(0, MARGIN, None)

    @pl.when(has_after)
    def _():
        up.wait_recv()
        place(MARGIN + tile, MARGIN, below)

    @pl.when(me == devices - 1)
    def _():
        place(MARGIN + tile, MARGIN, None)

    pl.when(has_before)(up.wait_send)
    pl.when(has_after)(down.wait_send)


def first_field(own):
    planes, parts, tile, width = own.shape
    vmem = pl.BlockSpec(memory_space=pltpu.VMEM)
    edge = pltpu.VMEM((planes, parts, MARGIN, width), jnp.float32)
    return pl.pallas_call(
        functools.partial(first_kernel, lax.axis_size("row")),
        out_shape=jax.ShapeDtypeStruct(
            (planes, parts, width // LANES, tile + 2 * MARGIN, LANES), jnp.float32
        ),
        in_specs=[vmem],
        out_specs=vmem,
        scratch_shapes=[edge, edge, pltpu.SemaphoreType.DMA((2,)), pltpu.SemaphoreType.DMA((2,))],
        compiler_params=pltpu.CompilerParams(
            collective_id=0, has_side_effects=True, vmem_limit_bytes=VMEM_LIMIT
        ),
    )(own)


def renew_kernel(
    devices, last, grad, sums, loss, field, probe, field_out, probe_out, loss_out,
    from_pair, loss_pair, to_peer, from_peer, renewed, above, below,
    pair_send, pair_recv, loss_sem, peer_send, peer_recv, spread_send, spread_recv,
    back_send, back_recv, edge_send, edge_recv,
):
    me = lax.axis_index("row")
    peers = devices // 2
    core, place = lax.rem(me, 2), lax.div(me, 2)
    partner = me + 1 - 2 * core
    piece = sums.shape[1] // devices
    extent = field.shape[3]
    reach = above.shape[3]
    has_before, has_after = me > 0, me < devices - 1

    def rows_of(side, index):
        return pl.ds(pl.multiple_of((side * peers + index) * piece, piece), piece)

    def to_pair(index, side):
        return send(
            sums.at[:, rows_of(side, index)], from_pair.at[index],
            pair_send.at[index], pair_recv.at[index], partner,
        )

    def to_place(index, slot):
        return send(
            to_peer.at[index], from_peer.at[slot],
            peer_send.at[index], peer_recv.at[slot], 2 * index + core,
        )

    def spread(index, slot):
        part = renewed.at[:, rows_of(core, slot)]
        return send(part, part, spread_send.at[index], spread_recv.at[slot], 2 * index + core)

    def back(index, side):
        part = renewed.at[:, rows_of(side, index)]
        return send(part, part, back_send.at[index], back_recv.at[index], partner)

    def after_me(step):
        return lax.rem(place + 1 + step, peers)

    def before_me(step):
        return lax.rem(place + peers - 1 - step, peers)

    other = me - 1 + 2 * core
    barrier = pltpu.get_barrier_semaphore()

    def signal(device):
        pl.semaphore_signal(barrier, inc=1, device_id={"row": device}, device_id_type=MESH)

    signal(partner)

    @pl.loop(0, peers - 1)
    def _(step):
        signal(2 * after_me(step) + core)

    beside = (other >= 0) & (other < devices)

    @pl.when(beside)
    def _():
        signal(other)

    pl.semaphore_wait(barrier, peers + beside.astype(jnp.int32))

    to_loss = send(loss, loss_pair, loss_sem.at[0], loss_sem.at[1], partner)
    to_loss.start()

    @pl.loop(0, peers)
    def _(step):
        to_pair(after_me(step), 1 - core).start()

    up = send(grad.at[:, :, :, pl.ds(0, reach)], below, edge_send.at[0], edge_recv.at[0], me - 1)
    down = send(
        grad.at[:, :, :, pl.ds(extent - reach, reach)], above, edge_send.at[1], edge_recv.at[1], me + 1
    )
    pl.when(core == 1)(up.start)
    pl.when(core == 0)(down.start)

    to_loss.wait()
    pair_loss = loss[...] + loss_pair[...]

    def add_pair(index):
        to_pair(index, core).wait_recv()
        both = sums[:, rows_of(core, index), :] + from_pair[index]
        return both

    @pl.loop(0, peers - 1)
    def _(step):
        index = after_me(step)
        both = add_pair(index)
        for plane in range(3):
            to_peer[index, plane * piece : (plane + 1) * piece] = both[plane]
        to_peer[index, 3 * piece :] = pair_loss
        to_place(index, place).start()

    both = add_pair(place)
    for plane in range(3):
        from_peer[place, plane * piece : (plane + 1) * piece] = both[plane]
    from_peer[place, 3 * piece :] = pair_loss

    square = probe[0] * probe[0] + probe[1] * probe[1]
    rate = OBJECT_RATE / (jnp.sum(square, keepdims=True) / (square.size) + TINY)

    @pl.loop(0, peers - 1)
    def _(step):
        index = before_me(step)
        to_place(index, index).wait_recv()

    total = from_peer[0]
    for index in range(1, peers):
        total = total + from_peer[index]
    loss_out[...] = total[3 * piece :]
    mine = rows_of(core, place)
    weight = total[2 * piece : 3 * piece] + DAMPING
    for part in range(2):
        step = PROBE_RATE * total[part * piece : (part + 1) * piece] / weight
        renewed[part, mine, :] = probe[part, mine, :] - step

    @pl.loop(0, peers - 1)
    def _(step):
        spread(after_me(step), place).start()

    back(place, core).start()
    pl.when((core == 0) & has_before)(up.start)
    pl.when((core == 1) & has_after)(down.start)

    first_row = MARGIN if last else 0
    planes = [
        (which, part, index)
        for which in range(grad.shape[0])
        for part in range(grad.shape[1])
        for index in range(grad.shape[2])
    ]

    def put(plane, start, value):
        rows = slice(start, start + value.shape[0])
        if last:
            which, part, index = plane
            field_out[which, part, rows, index * LANES : (index + 1) * LANES] = value
        else:
            field_out[(*plane, rows)] = value

    low, high = reach + first_row, extent - reach - first_row
    for plane in planes:
        rows = (*plane, slice(low, high))
        put(plane, reach, field[rows] - rate * grad[rows])

    @pl.loop(0, peers - 1)
    def _(step):
        index = before_me(step)
        spread(index, index).wait_recv()
        back(index, core).start()

    @pl.when(has_before)
    def _():
        down.wait_recv()

    @pl.when(me == 0)
    def _():
        above[...] = jnp.zeros_like(above)

    for plane in planes:
        rows = (*plane, slice(first_row, first_row + reach))
        put(plane, 0, field[rows] - rate * (grad[rows] + above[plane]))

    @pl.when(has_after)
    def _():
        up.wait_recv()

    @pl.when(me == devices - 1)
    def _():
        below[...] = jnp.zeros_like(below)

    for plane in planes:
        rows = (*plane, slice(extent - first_row - reach, extent - first_row))
        put(plane, extent - 2 * first_row - reach, field[rows] - rate * (grad[rows] + below[plane]))

    if not last:

        @pl.when(me == 0)
        def _():
            field_out[:, :, :, :MARGIN] = jnp.zeros((*field.shape[:3], MARGIN, LANES), jnp.float32)

        @pl.when(me == devices - 1)
        def _():
            field_out[:, :, :, extent - MARGIN :] = jnp.zeros(
                (*field.shape[:3], MARGIN, LANES), jnp.float32
            )

    @pl.loop(0, peers)
    def _(index):
        back(index, 1 - core).wait_recv()

    probe_out[...] = renewed[...]

    @pl.loop(0, peers)
    def _(index):
        to_pair(index, 1 - core).wait_send()
        back(index, core).wait_send()

    @pl.loop(0, peers - 1)
    def _(step):
        index = after_me(step)
        to_place(index, place).wait_send()
        spread(index, place).wait_send()

    pl.when(has_before)(up.wait_send)
    pl.when(has_after)(down.wait_send)


def renew(grad, sums, loss, field, probe, last):
    devices = lax.axis_size("row")
    peers = devices // 2
    planes, parts, tiles, extent, _ = field.shape
    piece = sums.shape[1] // devices
    reach = MARGIN if last else 2 * MARGIN
    shape = (planes, parts, extent - 2 * MARGIN, tiles * LANES) if last else field.shape
    vmem = pl.BlockSpec(memory_space=pltpu.VMEM)
    edge = pltpu.VMEM((planes, parts, tiles, reach, LANES), jnp.float32)
    packet = pltpu.VMEM((peers, 3 * piece + 8, LANES), jnp.float32)
    each = pltpu.SemaphoreType.DMA((peers,))
    two = pltpu.SemaphoreType.DMA((2,))
    return pl.pallas_call(
        functools.partial(renew_kernel, devices, last),
        out_shape=(
            jax.ShapeDtypeStruct(shape, jnp.float32),
            jax.ShapeDtypeStruct(probe.shape, jnp.float32),
            jax.ShapeDtypeStruct(loss.shape, jnp.float32),
        ),
        in_specs=[vmem] * 5,
        out_specs=(vmem,) * 3,
        scratch_shapes=[
            pltpu.VMEM((peers, 3, piece, LANES), jnp.float32),
            pltpu.VMEM(loss.shape, jnp.float32),
            packet,
            packet,
            pltpu.VMEM(probe.shape, jnp.float32),
            edge,
            edge,
            each, each, two, each, each, each, each, each, each, two, two,
        ],
        compiler_params=pltpu.CompilerParams(
            collective_id=2 if last else 1, has_side_effects=True, vmem_limit_bytes=VMEM_LIMIT
        ),
    )(grad, sums, loss, field, probe)


def shards(object_field, probe, intensity, row_offset, col_offset, slice_first):
    length = probe.shape[1]
    parts = length // LANES
    count = intensity.shape[0] * lax.axis_size("row") * length * length
    light = probe.reshape(2, length, parts, LANES).transpose(0, 2, 1, 3)
    light = light.reshape(2, parts * length, LANES)
    field = first_field(object_field)
    losses = []
    for step in range(ITERS):
        grad, sums, loss = local_terms(
            field, light, intensity, row_offset, col_offset, slice_first
        )
        field, light, loss = renew(grad, sums, loss, field, light, step == ITERS - 1)
        losses.append(jnp.sum(loss) / count)
    light = light.reshape(2, parts, length, LANES).transpose(0, 2, 1, 3)
    return field, light.reshape(probe.shape), jnp.stack(losses)


def solution(mesh):
    placed = (
        P("scan", None, "row", None),
        P("scan", None, None),
        P(("scan", "row"), None, None),
        P(("scan", "row")),
        P(("scan", "row")),
        P(("scan", "row")),
    )
    return jax.shard_map(
        shards,
        mesh=mesh,
        in_specs=placed,
        out_specs=(P("scan", None, "row", None), P("scan", None, None), P("scan")),
        check_vma=False,
    )
```

```python
import functools

import jax
import jax.numpy as jnp
import ml_dtypes
import numpy as np
from jax import lax
from jax.experimental import pallas as pl
from jax.experimental.pallas import tpu as pltpu
from jax.sharding import PartitionSpec as P

MARGIN = 64
ITERS = 2
SMOOTHING = 0.01
OBJECT_RATE = 0.25
PROBE_RATE = 0.5
PROPAGATION = 4.0
DAMPING = 1.0
TINY = 1e-06
LANES = 128
STRIP = 32
VMEM_LIMIT = 48 * 1024 * 1024
MESH = pl.DeviceIdType.MESH


def split_table(table):
    left = np.block([[table.real, -table.imag], [table.imag, table.real]])
    high = left.astype(ml_dtypes.bfloat16)
    low = (left - high.astype(np.float64)).astype(ml_dtypes.bfloat16)
    on_left = np.concatenate([high, low, high], axis=1)
    on_right = np.concatenate([high.T, high.T, low.T], axis=0)
    return np.ascontiguousarray(on_left), np.ascontiguousarray(on_right)


@functools.lru_cache(maxsize=None)
def tables(length):
    counter = np.arange(length)
    dft = np.exp(-2j * np.pi / length * ((counter[:, None] * counter[None, :]) % length))
    dft = dft / np.sqrt(length)
    signed = np.where(counter < length // 2, counter, counter - length) / length
    phase = np.exp(-1j * np.pi * PROPAGATION * signed**2)
    spread = (np.conj(dft) * phase[None, :]) @ dft
    return split_table(dft) + split_table(spread)


def joined(ref, plane, rows, length):
    return jnp.concatenate(
        [ref[plane, start + rows.start : start + rows.stop] for start in range(0, ref.shape[1], length)],
        axis=1,
    )


def times(a_re, a_im, b_re, b_im):
    return a_re * b_re - a_im * b_im, a_re * b_im + a_im * b_re


def local_kernel(
    rows_ref, cols_ref, first_ref, field, probe, intensity, dft_l, dft_r, spread_l, spread_r,
    grad, sums, loss, window, on_left, on_right, between, after, near,
):
    count, length = intensity.shape[:2]
    tiles = field.shape[2]
    strips = [slice(start, start + STRIP) for start in range(0, length, STRIP)]
    lane = lax.broadcasted_iota(jnp.int32, (STRIP, LANES), 1)
    row_at = [rows_ref[index] for index in range(count)]
    col_at = [cols_ref[index] for index in range(count)]
    front_at = [first_ref[index] for index in range(count)]

    def columns(index):
        return slice(index * length, (index + 1) * length)

    def set_left(index, rows, re, im):
        at = slice(index * length + rows.start, index * length + rows.stop)
        for value, start in ((re, 0), (im, length)):
            high = value.astype(jnp.bfloat16)
            low = (value - high.astype(jnp.float32)).astype(jnp.bfloat16)
            on_left[at, start : start + length] = high
            on_left[at, start + 2 * length : start + 3 * length] = low
            on_left[at, start + 4 * length : start + 5 * length] = high

    def both_sides(table_l, table_r):
        between[...] = jnp.dot(on_left[...], table_r[...], preferred_element_type=jnp.float32)
        for index in range(count):
            for rows in strips:
                at = slice(index * length + rows.start, index * length + rows.stop)
                for start in (0, length):
                    value = between[at, start : start + length]
                    high = value.astype(jnp.bfloat16)
                    low = (value - high.astype(jnp.float32)).astype(jnp.bfloat16)
                    for base, piece in ((0, high), (2 * length, high), (4 * length, low)):
                        first = base + start + rows.start
                        on_right[first : first + STRIP, columns(index)] = piece
        after[...] = jnp.dot(table_l[...], on_right[...], preferred_element_type=jnp.float32)

    def result(index, rows):
        below = slice(length + rows.start, length + rows.stop)
        return after[rows, columns(index)], after[below, columns(index)]

    grad[...] = jnp.zeros_like(grad)
    for index in range(count):
        back = lax.rem(LANES - col_at[index], LANES)
        stays = lane < LANES - col_at[index]
        for rows in strips:
            taken = pl.ds(row_at[index] + rows.start, STRIP)
            for which, source in ((0, front_at[index]), (1, 1 - front_at[index])):
                for part in range(2):
                    rolled = [
                        pltpu.roll(field[source, part, tile, taken, :], back, 1)
                        for tile in range(tiles)
                    ]
                    for tile in range(tiles - 1):
                        window[index, which, part, rows, tile * LANES : (tile + 1) * LANES] = (
                            jnp.where(stays, rolled[tile], rolled[tile + 1])
                        )
            front_re, front_im = window[index, 0, 0, rows], window[index, 0, 1, rows]
            light_re, light_im = joined(probe, 0, rows, length), joined(probe, 1, rows, length)
            set_left(index, rows, *times(light_re, light_im, front_re, front_im))

    both_sides(spread_l, spread_r)
    for index in range(count):
        for rows in strips:
            near_re, near_im = result(index, rows)
            near[index, 0, rows] = near_re
            near[index, 1, rows] = near_im
            behind_re, behind_im = window[index, 1, 0, rows], window[index, 1, 1, rows]
            set_left(index, rows, *times(near_re, near_im, behind_re, behind_im))

    both_sides(dft_l, dft_r)
    total = jnp.zeros((8, length), jnp.float32)
    for index in range(count):
        for rows in strips:
            far_re, far_im = result(index, rows)
            power = far_re * far_re + far_im * far_im + SMOOTHING
            modulus = jnp.sqrt(power)
            misfit = modulus - jnp.sqrt(intensity[index, rows] + SMOOTHING)
            total += jnp.sum((misfit * misfit).reshape(STRIP // 8, 8, length), axis=0)
            slope = 2.0 * misfit / modulus
            set_left(index, rows, slope * far_re, -slope * far_im)
    loss[...] = sum(
        total[:, start : start + LANES] for start in range(0, length, LANES)
    )

    def scatter(index, rows, source, part, value):
        col = lax.rem(col_at[index], LANES)
        moved = lane < col_at[index]
        taken = pl.ds(row_at[index] + rows.start, STRIP)
        rolled = [
            pltpu.roll(value[:, tile * LANES : (tile + 1) * LANES], col, 1)
            for tile in range(tiles - 1)
        ]
        zero = jnp.zeros_like(rolled[0])
        for tile in range(tiles):
            here = rolled[tile] if tile < tiles - 1 else zero
            ahead = rolled[tile - 1] if tile else zero
            grad[source, part, tile, taken, :] += jnp.where(moved, ahead, here)

    both_sides(dft_l, dft_r)
    for index in range(count):
        for rows in strips:
            exit_re, exit_im = result(index, rows)
            behind_re, behind_im = window[index, 1, 0, rows], window[index, 1, 1, rows]
            set_left(index, rows, *times(behind_re, behind_im, exit_re, exit_im))
            grad_re, grad_im = times(near[index, 0, rows], near[index, 1, rows], exit_re, exit_im)
            scatter(index, rows, 1 - front_at[index], 0, grad_re)
            scatter(index, rows, 1 - front_at[index], 1, -grad_im)

    both_sides(spread_l, spread_r)
    for rows in strips:
        light_re, light_im = joined(probe, 0, rows, length), joined(probe, 1, rows, length)
        planes = [jnp.zeros((STRIP, length), jnp.float32)] * 3
        for index in range(count):
            wave_re, wave_im = result(index, rows)
            front_re, front_im = window[index, 0, 0, rows], window[index, 0, 1, rows]
            probe_re, probe_im = times(front_re, front_im, wave_re, wave_im)
            planes[0] += probe_re
            planes[1] -= probe_im
            planes[2] += front_re * front_re + front_im * front_im
            grad_re, grad_im = times(light_re, light_im, wave_re, wave_im)
            scatter(index, rows, front_at[index], 0, grad_re)
            scatter(index, rows, front_at[index], 1, -grad_im)
        for plane, value in enumerate(planes):
            for part in range(length // LANES):
                at = slice(part * length + rows.start, part * length + rows.stop)
                sums[plane, at] = value[:, part * LANES : (part + 1) * LANES]


def local_terms(field, probe, intensity, rows, cols, first):
    count, length = intensity.shape[:2]
    vmem = pl.BlockSpec(memory_space=pltpu.VMEM)
    smem = pl.BlockSpec(memory_space=pltpu.SMEM)
    return pl.pallas_call(
        local_kernel,
        out_shape=(
            jax.ShapeDtypeStruct(field.shape, jnp.float32),
            jax.ShapeDtypeStruct((3, length * length // LANES, LANES), jnp.float32),
            jax.ShapeDtypeStruct((8, LANES), jnp.float32),
        ),
        in_specs=[smem] * 3 + [vmem] * 7,
        out_specs=(vmem,) * 3,
        scratch_shapes=[
            pltpu.VMEM((count, 2, 2, length, length), jnp.float32),
            pltpu.VMEM((count * length, 6 * length), jnp.bfloat16),
            pltpu.VMEM((6 * length, count * length), jnp.bfloat16),
            pltpu.VMEM((count * length, 2 * length), jnp.float32),
            pltpu.VMEM((2 * length, count * length), jnp.float32),
            pltpu.VMEM((count, 2, length, length), jnp.float32),
        ],
        compiler_params=pltpu.CompilerParams(vmem_limit_bytes=VMEM_LIMIT),
    )(rows, cols, first, field, probe, intensity, *(jnp.asarray(t) for t in tables(length)))


def greet(devices):
    barrier = pltpu.get_barrier_semaphore()
    for condition, device in devices:

        @pl.when(condition)
        def _(device=device):
            pl.semaphore_signal(barrier, inc=1, device_id={"row": device}, device_id_type=MESH)

    pl.semaphore_wait(barrier, sum(condition.astype(jnp.int32) for condition, _ in devices))


def send(source, target, send_sem, recv_sem, device):
    return pltpu.make_async_remote_copy(
        src_ref=source,
        dst_ref=target,
        send_sem=send_sem,
        recv_sem=recv_sem,
        device_id={"row": device},
        device_id_type=MESH,
    )


def first_kernel(
    devices, own, probe, field, light, above, below, send_sem, recv_sem
):
    me = lax.axis_index("row")
    tile = own.shape[2]
    has_before, has_after = me > 0, me < devices - 1
    greet(((has_before, me - 1), (has_after, me + 1)))
    up = send(own.at[:, :, pl.ds(0, MARGIN)], below, send_sem.at[0], recv_sem.at[0], me - 1)
    down = send(
        own.at[:, :, pl.ds(tile - MARGIN, MARGIN)], above, send_sem.at[1], recv_sem.at[1], me + 1
    )
    pl.when(has_before)(up.start)
    pl.when(has_after)(down.start)

    def place(start, rows, source):
        for index in range(field.shape[2]):
            columns = slice(index * LANES, (index + 1) * LANES)
            field[:, :, index, start : start + rows] = (
                jnp.zeros((2, 2, rows, LANES), jnp.float32)
                if source is None
                else source[:, :, :, columns]
            )

    place(MARGIN, tile, own)
    length = probe.shape[1]
    for part in range(length // LANES):
        columns = slice(part * LANES, (part + 1) * LANES)
        light[:, part * length : (part + 1) * length] = probe[:, :, columns]

    @pl.when(has_before)
    def _():
        down.wait_recv()
        place(0, MARGIN, above)

    @pl.when(me == 0)
    def _():
        place(0, MARGIN, None)

    @pl.when(has_after)
    def _():
        up.wait_recv()
        place(MARGIN + tile, MARGIN, below)

    @pl.when(me == devices - 1)
    def _():
        place(MARGIN + tile, MARGIN, None)

    pl.when(has_before)(up.wait_send)
    pl.when(has_after)(down.wait_send)


def first_field(own, probe):
    planes, parts, tile, width = own.shape
    vmem = pl.BlockSpec(memory_space=pltpu.VMEM)
    edge = pltpu.VMEM((planes, parts, MARGIN, width), jnp.float32)
    return pl.pallas_call(
        functools.partial(first_kernel, lax.axis_size("row")),
        out_shape=(
            jax.ShapeDtypeStruct(
                (planes, parts, width // LANES, tile + 2 * MARGIN, LANES), jnp.float32
            ),
            jax.ShapeDtypeStruct((2, probe[0].size // LANES, LANES), jnp.float32),
        ),
        in_specs=[vmem] * 2,
        out_specs=(vmem,) * 2,
        scratch_shapes=[edge, edge, pltpu.SemaphoreType.DMA((2,)), pltpu.SemaphoreType.DMA((2,))],
        compiler_params=pltpu.CompilerParams(
            collective_id=0, has_side_effects=True, vmem_limit_bytes=VMEM_LIMIT
        ),
    )(own, probe)


def object_rate(probe):
    square = probe[0] * probe[0] + probe[1] * probe[1]
    return OBJECT_RATE / (jnp.sum(square, keepdims=True) / square.size + TINY)


def planes_of(ref):
    first, second, third = ref.shape[:3]
    return [(i, j, k) for i in range(first) for j in range(second) for k in range(third)]


def renew_kernel(devices, last, grad, sums, loss, probe, *refs):
    if last:
        above_out, below_out, probe_out, loss_out, *refs = refs
    else:
        field, field_out, probe_out, loss_out, *refs = refs
    (
        from_pair, loss_of, to_mate, from_mate, to_peer, from_peer, renewed, above, below,
        loss_send, loss_recv, pair_send, pair_recv, mate_send, mate_recv, peer_send, peer_recv,
        spread_send, spread_recv, cross_send, cross_recv, back_send, back_recv,
        edge_send, edge_recv,
    ) = refs
    me = lax.axis_index("row")
    peers = devices // 4
    core, side, place = lax.rem(me, 2), lax.rem(lax.div(me, 2), 2), lax.div(me, 4)
    partner, mate = me + 1 - 2 * core, me + 2 - 4 * side
    piece = sums.shape[1] // devices
    extent = grad.shape[3]
    reach = above.shape[3]
    has_before, has_after = me > 0, me < devices - 1

    def rows_of(core_at, side_at, index):
        start = ((core_at * 2 + side_at) * peers + index) * piece
        return pl.ds(pl.multiple_of(start, piece), piece)

    def to_pair(side_at, index, core_at):
        return send(
            sums.at[:, rows_of(core_at, side_at, index)], from_pair.at[side_at, index],
            pair_send.at[side_at, index], pair_recv.at[side_at, index], partner,
        )

    def to_side(index):
        return send(
            to_mate.at[index], from_mate.at[index], mate_send.at[index], mate_recv.at[index], mate
        )

    def to_place(index, slot):
        return send(
            to_peer.at[index], from_peer.at[slot],
            peer_send.at[index], peer_recv.at[slot], 4 * index + 2 * side + core,
        )

    def spread(index, slot):
        part = renewed.at[:, rows_of(core, side, slot)]
        return send(
            part, part, spread_send.at[index], spread_recv.at[slot], 4 * index + 2 * side + core
        )

    def cross(side_at, index):
        part = renewed.at[:, rows_of(core, side_at, index)]
        return send(part, part, cross_send.at[index], cross_recv.at[index], mate)

    def back(core_at, side_at, index):
        part = renewed.at[:, rows_of(core_at, side_at, index)]
        return send(
            part, part, back_send.at[side_at, index], back_recv.at[side_at, index], partner
        )

    def after_me(step):
        return lax.rem(place + 1 + step, peers)

    def before_me(step):
        return lax.rem(place + peers - 1 - step, peers)

    other = me - 1 + 2 * core
    beside = (other >= 0) & (other < devices)
    barrier = pltpu.get_barrier_semaphore()

    def signal(device):
        pl.semaphore_signal(barrier, inc=1, device_id={"row": device}, device_id_type=MESH)

    signal(partner)
    signal(mate)

    @pl.loop(0, peers - 1)
    def _(step):
        signal(4 * after_me(step) + 2 * side + core)

    @pl.when(beside)
    def _():
        signal(other)

    pl.semaphore_wait(barrier, peers + 1 + beside.astype(jnp.int32))

    pair_loss = send(loss, loss_of.at[0], loss_send.at[0], loss_recv.at[0], partner)
    mate_loss = send(loss_of.at[1], loss_of.at[2], loss_send.at[1], loss_recv.at[1], mate)
    pair_loss.start()

    @pl.loop(0, peers)
    def _(step):
        to_pair(1 - side, after_me(step), 1 - core).start()

    @pl.loop(0, peers)
    def _(step):
        to_pair(side, after_me(step), 1 - core).start()

    up = send(
        grad.at[:, :, :, pl.ds(0, reach)], below, edge_send.at[0], edge_recv.at[0], me - 1
    )
    down = send(
        grad.at[:, :, :, pl.ds(extent - reach, reach)], above,
        edge_send.at[1], edge_recv.at[1], me + 1,
    )

    pair_loss.wait()
    loss_of[1] = loss[...] + loss_of[0]
    mate_loss.start()

    def add_pair(side_at, index):
        to_pair(side_at, index, core).wait_recv()
        return sums[:, rows_of(core, side_at, index), :] + from_pair[side_at, index]

    @pl.loop(0, peers)
    def _(step):
        index = after_me(step)
        to_mate[index] = add_pair(1 - side, index)
        to_side(index).start()

    pl.when(has_before)(up.start)
    pl.when(has_after)(down.start)

    mate_loss.wait()
    quad_loss = loss_of[1] + loss_of[2]

    def fill(target, slot, index):
        both = add_pair(side, index)
        to_side(index).wait_recv()
        both = both + from_mate[index]
        for plane in range(3):
            target[slot, plane * piece : (plane + 1) * piece] = both[plane]
        target[slot, 3 * piece :] = quad_loss

    @pl.loop(0, peers - 1)
    def _(step):
        index = after_me(step)
        fill(to_peer, index, index)
        to_place(index, place).start()

    fill(from_peer, place, place)

    rate = object_rate(probe)

    @pl.loop(0, peers - 1)
    def _(step):
        index = before_me(step)
        to_place(index, index).wait_recv()

    total = from_peer[0]
    for index in range(1, peers):
        total = total + from_peer[index]
    loss_out[...] = total[3 * piece :]
    mine = rows_of(core, side, place)
    weight = total[2 * piece : 3 * piece] + DAMPING
    for part in range(2):
        step = PROBE_RATE * total[part * piece : (part + 1) * piece] / weight
        renewed[part, mine, :] = probe[part, mine, :] - step

    @pl.loop(0, peers - 1)
    def _(step):
        spread(after_me(step), place).start()

    cross(side, place).start()
    back(core, side, place).start()

    if not last:
        for plane in planes_of(grad):
            rows = (*plane, slice(reach, extent - reach))
            field_out[rows] = field[rows] - rate * grad[rows]

    @pl.loop(0, peers - 1)
    def _(step):
        index = before_me(step)
        spread(index, index).wait_recv()
        cross(side, index).start()
        back(core, side, index).start()

    @pl.loop(0, peers)
    def _(step):
        index = lax.rem(place + peers - step, peers)
        cross(1 - side, index).wait_recv()
        back(core, 1 - side, index).start()

    @pl.when(has_before)
    def _():
        down.wait_recv()

    @pl.when(me == 0)
    def _():
        above[...] = jnp.zeros_like(above)

    if last:
        above_out[...] = above[...]
    else:
        for plane in planes_of(grad):
            rows = (*plane, slice(0, reach))
            field_out[rows] = field[rows] - rate * (grad[rows] + above[plane])

    @pl.when(has_after)
    def _():
        up.wait_recv()

    @pl.when(me == devices - 1)
    def _():
        below[...] = jnp.zeros_like(below)

    if last:
        below_out[...] = below[...]
    else:
        for plane in planes_of(grad):
            rows = (*plane, slice(extent - reach, extent))
            field_out[rows] = field[rows] - rate * (grad[rows] + below[plane])
        empty = (*field.shape[:3], MARGIN, LANES)

        @pl.when(me == 0)
        def _():
            field_out[:, :, :, :MARGIN] = jnp.zeros(empty, jnp.float32)

        @pl.when(me == devices - 1)
        def _():
            field_out[:, :, :, extent - MARGIN :] = jnp.zeros(empty, jnp.float32)

    for side_at in range(2):

        @pl.loop(0, peers)
        def _(index, side_at=side_at):
            back(1 - core, side_at, index).wait_recv()

    probe_out[...] = renewed[...]

    for side_at in range(2):

        @pl.loop(0, peers)
        def _(index, side_at=side_at):
            to_pair(side_at, index, 1 - core).wait_send()
            back(core, side_at, index).wait_send()

    @pl.loop(0, peers)
    def _(index):
        to_side(index).wait_send()
        cross(side, index).wait_send()

    @pl.loop(0, peers - 1)
    def _(step):
        index = after_me(step)
        to_place(index, place).wait_send()
        spread(index, place).wait_send()

    pl.when(has_before)(up.wait_send)
    pl.when(has_after)(down.wait_send)


def renew(grad, sums, loss, field, probe, last):
    devices = lax.axis_size("row")
    peers = devices // 4
    piece = sums.shape[1] // devices
    reach = MARGIN if last else 2 * MARGIN
    vmem = pl.BlockSpec(memory_space=pltpu.VMEM)
    edge_shape = (*field.shape[:3], reach, LANES)
    edge = pltpu.VMEM(edge_shape, jnp.float32)
    edge_out = jax.ShapeDtypeStruct(edge_shape, jnp.float32)
    packet = pltpu.VMEM((peers, 3 * piece + 8, LANES), jnp.float32)
    part = pltpu.VMEM((peers, 3, piece, LANES), jnp.float32)
    each = pltpu.SemaphoreType.DMA((peers,))
    double = pltpu.SemaphoreType.DMA((2, peers))
    two = pltpu.SemaphoreType.DMA((2,))
    objects = (edge_out, edge_out) if last else (jax.ShapeDtypeStruct(field.shape, jnp.float32),)
    outs = objects + (
        jax.ShapeDtypeStruct(probe.shape, jnp.float32),
        jax.ShapeDtypeStruct(loss.shape, jnp.float32),
    )
    operands = (grad, sums, loss, probe) + (() if last else (field,))
    return pl.pallas_call(
        functools.partial(renew_kernel, devices, last),
        out_shape=outs,
        in_specs=[vmem] * len(operands),
        out_specs=(vmem,) * len(outs),
        scratch_shapes=[
            pltpu.VMEM((2, peers, 3, piece, LANES), jnp.float32),
            pltpu.VMEM((3, *loss.shape), jnp.float32),
            part,
            part,
            packet,
            packet,
            pltpu.VMEM(probe.shape, jnp.float32),
            edge,
            edge,
            two, two, double, double, each, each, each, each,
            each, each, each, each, double, double,
            two, two,
        ],
        compiler_params=pltpu.CompilerParams(
            collective_id=2 if last else 1, has_side_effects=True, vmem_limit_bytes=VMEM_LIMIT
        ),
    )(*operands)


def finish_kernel(
    count, field, grad, above, below, old, probe, *refs
):
    *losses, field_out, probe_out, misfit_out = refs
    rate = object_rate(old)
    length = probe_out.shape[1]
    tile = field_out.shape[2]
    for plane in planes_of(field):
        which, part, index = plane
        columns = slice(index * LANES, (index + 1) * LANES)
        for start, stop, extra in (
            (0, MARGIN, above), (MARGIN, tile - MARGIN, None), (tile - MARGIN, tile, below)
        ):
            rows = (*plane, slice(MARGIN + start, MARGIN + stop))
            value = grad[rows] if extra is None else grad[rows] + extra[plane]
            field_out[which, part, start:stop, columns] = field[rows] - rate * value
    for part in range(length // LANES):
        columns = slice(part * LANES, (part + 1) * LANES)
        probe_out[:, :, columns] = probe[:, part * length : (part + 1) * length]
    for index, loss in enumerate(losses):
        misfit_out[index] = jnp.sum(loss[...]) / count


def finish(count, field, grad, above, below, old, probe, losses, shapes):
    vmem = pl.BlockSpec(memory_space=pltpu.VMEM)
    return pl.pallas_call(
        functools.partial(finish_kernel, count),
        out_shape=tuple(
            jax.ShapeDtypeStruct(shape, jnp.float32) for shape in (*shapes, (len(losses),))
        ),
        in_specs=[vmem] * (6 + len(losses)),
        out_specs=(vmem, vmem, pl.BlockSpec(memory_space=pltpu.SMEM)),
        compiler_params=pltpu.CompilerParams(vmem_limit_bytes=VMEM_LIMIT),
    )(field, grad, above, below, old, probe, *losses)


def shards(object_field, probe, intensity, row_offset, col_offset, slice_first):
    length = probe.shape[1]
    count = float(intensity.shape[0] * lax.axis_size("row") * length * length)
    field, light = first_field(object_field, probe)
    losses = []
    for step in range(ITERS):
        grad, sums, loss = local_terms(
            field, light, intensity, row_offset, col_offset, slice_first
        )
        old = light
        if step < ITERS - 1:
            field, light, loss = renew(grad, sums, loss, field, light, False)
        else:
            above, below, light, loss = renew(grad, sums, loss, field, light, True)
        losses.append(loss)
    shapes = (object_field.shape, probe.shape)
    return finish(count, field, grad, above, below, old, light, losses, shapes)


def solution(mesh):
    placed = (
        P("scan", None, "row", None),
        P("scan", None, None),
        P(("scan", "row"), None, None),
        P(("scan", "row")),
        P(("scan", "row")),
        P(("scan", "row")),
    )
    return jax.shard_map(
        shards,
        mesh=mesh,
        in_specs=placed,
        out_specs=(P("scan", None, "row", None), P("scan", None, None), P("scan")),
        check_vma=False,
    )
```

```python
import functools

import jax
import jax.numpy as jnp
import ml_dtypes
import numpy as np
from jax import lax
from jax.experimental import pallas as pl
from jax.experimental.pallas import tpu as pltpu
from jax.sharding import PartitionSpec as P

MARGIN = 64
ITERS = 2
SMOOTHING = 0.01
OBJECT_RATE = 0.25
PROBE_RATE = 0.5
PROPAGATION = 4.0
DAMPING = 1.0
TINY = 1e-06
LANES = 128
STRIP = 32
VMEM_LIMIT = 24 * 1024 * 1024
MESH = pl.DeviceIdType.MESH


def split_table(table):
    left = np.block([[table.real, -table.imag], [table.imag, table.real]])
    high = left.astype(ml_dtypes.bfloat16)
    low = (left - high.astype(np.float64)).astype(ml_dtypes.bfloat16)
    on_left = np.concatenate([high, low, high], axis=1)
    on_right = np.concatenate([high.T, high.T, low.T], axis=0)
    return np.ascontiguousarray(on_left), np.ascontiguousarray(on_right)


@functools.lru_cache(maxsize=None)
def tables(length):
    counter = np.arange(length)
    dft = np.exp(-2j * np.pi / length * ((counter[:, None] * counter[None, :]) % length))
    dft = dft / np.sqrt(length)
    signed = np.where(counter < length // 2, counter, counter - length) / length
    phase = np.exp(-1j * np.pi * PROPAGATION * signed**2)
    spread = (np.conj(dft) * phase[None, :]) @ dft
    return split_table(dft) + split_table(spread)


def joined(ref, plane, rows, length):
    return jnp.concatenate(
        [ref[plane, start + rows.start : start + rows.stop] for start in range(0, ref.shape[1], length)],
        axis=1,
    )


def times(a_re, a_im, b_re, b_im):
    return a_re * b_re - a_im * b_im, a_re * b_im + a_im * b_re


def local_kernel(
    rows_ref, cols_ref, first_ref, field, probe, intensity, dft_l, dft_r, spread_l, spread_r,
    grad, sums, loss, window, on_left, on_right, between, after, near,
):
    count, length = intensity.shape[:2]
    tiles = field.shape[2]
    strips = [slice(start, start + STRIP) for start in range(0, length, STRIP)]
    lane = lax.broadcasted_iota(jnp.int32, (STRIP, LANES), 1)
    row_at = [rows_ref[index] for index in range(count)]
    col_at = [cols_ref[index] for index in range(count)]
    front_at = [first_ref[index] for index in range(count)]

    def columns(index):
        return slice(index * length, (index + 1) * length)

    def set_left(index, rows, re, im):
        at = slice(index * length + rows.start, index * length + rows.stop)
        for value, start in ((re, 0), (im, length)):
            high = value.astype(jnp.bfloat16)
            low = (value - high.astype(jnp.float32)).astype(jnp.bfloat16)
            on_left[at, start : start + length] = high
            on_left[at, start + 2 * length : start + 3 * length] = low
            on_left[at, start + 4 * length : start + 5 * length] = high

    def both_sides(table_l, table_r):
        between[...] = jnp.dot(on_left[...], table_r[...], preferred_element_type=jnp.float32)
        for index in range(count):
            for rows in strips:
                at = slice(index * length + rows.start, index * length + rows.stop)
                for start in (0, length):
                    value = between[at, start : start + length]
                    high = value.astype(jnp.bfloat16)
                    low = (value - high.astype(jnp.float32)).astype(jnp.bfloat16)
                    for base, piece in ((0, high), (2 * length, high), (4 * length, low)):
                        first = base + start + rows.start
                        on_right[first : first + STRIP, columns(index)] = piece
        after[...] = jnp.dot(table_l[...], on_right[...], preferred_element_type=jnp.float32)

    def result(index, rows):
        below = slice(length + rows.start, length + rows.stop)
        return after[rows, columns(index)], after[below, columns(index)]

    grad[...] = jnp.zeros_like(grad)
    for index in range(count):
        back = lax.rem(LANES - col_at[index], LANES)
        stays = lane < LANES - col_at[index]
        for rows in strips:
            taken = pl.ds(row_at[index] + rows.start, STRIP)
            for which, source in ((0, front_at[index]), (1, 1 - front_at[index])):
                for part in range(2):
                    rolled = [
                        pltpu.roll(field[source, part, tile, taken, :], back, 1)
                        for tile in range(tiles)
                    ]
                    for tile in range(tiles - 1):
                        window[index, which, part, rows, tile * LANES : (tile + 1) * LANES] = (
                            jnp.where(stays, rolled[tile], rolled[tile + 1])
                        )
            front_re, front_im = window[index, 0, 0, rows], window[index, 0, 1, rows]
            light_re, light_im = joined(probe, 0, rows, length), joined(probe, 1, rows, length)
            set_left(index, rows, *times(light_re, light_im, front_re, front_im))

    both_sides(spread_l, spread_r)
    for index in range(count):
        for rows in strips:
            near_re, near_im = result(index, rows)
            near[index, 0, rows] = near_re
            near[index, 1, rows] = near_im
            behind_re, behind_im = window[index, 1, 0, rows], window[index, 1, 1, rows]
            set_left(index, rows, *times(near_re, near_im, behind_re, behind_im))

    both_sides(dft_l, dft_r)
    total = jnp.zeros((8, length), jnp.float32)
    for index in range(count):
        for rows in strips:
            far_re, far_im = result(index, rows)
            power = far_re * far_re + far_im * far_im + SMOOTHING
            modulus = jnp.sqrt(power)
            misfit = modulus - jnp.sqrt(intensity[index, rows] + SMOOTHING)
            total += jnp.sum((misfit * misfit).reshape(STRIP // 8, 8, length), axis=0)
            slope = 2.0 * misfit / modulus
            set_left(index, rows, slope * far_re, -slope * far_im)
    loss[...] = sum(
        total[:, start : start + LANES] for start in range(0, length, LANES)
    )

    def scatter(index, rows, source, part, value):
        col = lax.rem(col_at[index], LANES)
        moved = lane < col_at[index]
        taken = pl.ds(row_at[index] + rows.start, STRIP)
        rolled = [
            pltpu.roll(value[:, tile * LANES : (tile + 1) * LANES], col, 1)
            for tile in range(tiles - 1)
        ]
        zero = jnp.zeros_like(rolled[0])
        for tile in range(tiles):
            here = rolled[tile] if tile < tiles - 1 else zero
            ahead = rolled[tile - 1] if tile else zero
            grad[source, part, tile, taken, :] += jnp.where(moved, ahead, here)

    both_sides(dft_l, dft_r)
    for index in range(count):
        for rows in strips:
            exit_re, exit_im = result(index, rows)
            behind_re, behind_im = window[index, 1, 0, rows], window[index, 1, 1, rows]
            set_left(index, rows, *times(behind_re, behind_im, exit_re, exit_im))
            grad_re, grad_im = times(near[index, 0, rows], near[index, 1, rows], exit_re, exit_im)
            scatter(index, rows, 1 - front_at[index], 0, grad_re)
            scatter(index, rows, 1 - front_at[index], 1, -grad_im)

    both_sides(spread_l, spread_r)
    for rows in strips:
        light_re, light_im = joined(probe, 0, rows, length), joined(probe, 1, rows, length)
        planes = [jnp.zeros((STRIP, length), jnp.float32)] * 3
        for index in range(count):
            wave_re, wave_im = result(index, rows)
            front_re, front_im = window[index, 0, 0, rows], window[index, 0, 1, rows]
            probe_re, probe_im = times(front_re, front_im, wave_re, wave_im)
            planes[0] += probe_re
            planes[1] -= probe_im
            planes[2] += front_re * front_re + front_im * front_im
            grad_re, grad_im = times(light_re, light_im, wave_re, wave_im)
            scatter(index, rows, front_at[index], 0, grad_re)
            scatter(index, rows, front_at[index], 1, -grad_im)
        for plane, value in enumerate(planes):
            for part in range(length // LANES):
                at = slice(part * length + rows.start, part * length + rows.stop)
                sums[plane, at] = value[:, part * LANES : (part + 1) * LANES]


def local_terms(field, probe, intensity, rows, cols, first):
    count, length = intensity.shape[:2]
    vmem = pl.BlockSpec(memory_space=pltpu.VMEM)
    smem = pl.BlockSpec(memory_space=pltpu.SMEM)
    return pl.pallas_call(
        local_kernel,
        out_shape=(
            jax.ShapeDtypeStruct(field.shape, jnp.float32),
            jax.ShapeDtypeStruct((3, length * length // LANES, LANES), jnp.float32),
            jax.ShapeDtypeStruct((8, LANES), jnp.float32),
        ),
        in_specs=[smem] * 3 + [vmem] * 7,
        out_specs=(vmem,) * 3,
        scratch_shapes=[
            pltpu.VMEM((count, 2, 2, length, length), jnp.float32),
            pltpu.VMEM((count * length, 6 * length), jnp.bfloat16),
            pltpu.VMEM((6 * length, count * length), jnp.bfloat16),
            pltpu.VMEM((count * length, 2 * length), jnp.float32),
            pltpu.VMEM((2 * length, count * length), jnp.float32),
            pltpu.VMEM((count, 2, length, length), jnp.float32),
        ],
        compiler_params=pltpu.CompilerParams(vmem_limit_bytes=VMEM_LIMIT),
    )(rows, cols, first, field, probe, intensity, *(jnp.asarray(t) for t in tables(length)))


def greet(devices):
    barrier = pltpu.get_barrier_semaphore()
    for condition, device in devices:

        @pl.when(condition)
        def _(device=device):
            pl.semaphore_signal(barrier, inc=1, device_id={"row": device}, device_id_type=MESH)

    pl.semaphore_wait(barrier, sum(condition.astype(jnp.int32) for condition, _ in devices))


def send(source, target, send_sem, recv_sem, device):
    return pltpu.make_async_remote_copy(
        src_ref=source,
        dst_ref=target,
        send_sem=send_sem,
        recv_sem=recv_sem,
        device_id={"row": device},
        device_id_type=MESH,
    )


def first_kernel(
    devices, own, probe, field, light, above, below, send_sem, recv_sem
):
    me = lax.axis_index("row")
    tile = own.shape[2]
    has_before, has_after = me > 0, me < devices - 1
    greet(((has_before, me - 1), (has_after, me + 1)))
    up = send(own.at[:, :, pl.ds(0, MARGIN)], below, send_sem.at[0], recv_sem.at[0], me - 1)
    down = send(
        own.at[:, :, pl.ds(tile - MARGIN, MARGIN)], above, send_sem.at[1], recv_sem.at[1], me + 1
    )
    pl.when(has_before)(up.start)
    pl.when(has_after)(down.start)

    def place(start, rows, source):
        for index in range(field.shape[2]):
            columns = slice(index * LANES, (index + 1) * LANES)
            field[:, :, index, start : start + rows] = (
                jnp.zeros((2, 2, rows, LANES), jnp.float32)
                if source is None
                else source[:, :, :, columns]
            )

    place(MARGIN, tile, own)
    length = probe.shape[1]
    for part in range(length // LANES):
        columns = slice(part * LANES, (part + 1) * LANES)
        light[:, part * length : (part + 1) * length] = probe[:, :, columns]

    @pl.when(has_before)
    def _():
        down.wait_recv()
        place(0, MARGIN, above)

    @pl.when(me == 0)
    def _():
        place(0, MARGIN, None)

    @pl.when(has_after)
    def _():
        up.wait_recv()
        place(MARGIN + tile, MARGIN, below)

    @pl.when(me == devices - 1)
    def _():
        place(MARGIN + tile, MARGIN, None)

    pl.when(has_before)(up.wait_send)
    pl.when(has_after)(down.wait_send)


def first_field(own, probe):
    planes, parts, tile, width = own.shape
    vmem = pl.BlockSpec(memory_space=pltpu.VMEM)
    edge = pltpu.VMEM((planes, parts, MARGIN, width), jnp.float32)
    return pl.pallas_call(
        functools.partial(first_kernel, lax.axis_size("row")),
        out_shape=(
            jax.ShapeDtypeStruct(
                (planes, parts, width // LANES, tile + 2 * MARGIN, LANES), jnp.float32
            ),
            jax.ShapeDtypeStruct((2, probe[0].size // LANES, LANES), jnp.float32),
        ),
        in_specs=[vmem] * 2,
        out_specs=(vmem,) * 2,
        scratch_shapes=[edge, edge, pltpu.SemaphoreType.DMA((2,)), pltpu.SemaphoreType.DMA((2,))],
        compiler_params=pltpu.CompilerParams(
            collective_id=0, has_side_effects=True, vmem_limit_bytes=VMEM_LIMIT
        ),
    )(own, probe)


def object_rate(probe):
    square = probe[0] * probe[0] + probe[1] * probe[1]
    return OBJECT_RATE / (jnp.sum(square, keepdims=True) / square.size + TINY)


def planes_of(ref):
    first, second, third = ref.shape[:3]
    return [(i, j, k) for i in range(first) for j in range(second) for k in range(third)]


def renew_kernel(devices, last, grad, sums, loss, probe, *refs):
    if last:
        above_out, below_out, probe_out, loss_out, *refs = refs
    else:
        field, field_out, probe_out, loss_out, *refs = refs
    (
        from_pair, loss_of, to_mate, from_mate, to_peer, from_peer, renewed, above, below,
        loss_send, loss_recv, pair_send, pair_recv, mate_send, mate_recv, peer_send, peer_recv,
        spread_send, spread_recv, cross_send, cross_recv, back_send, back_recv,
        edge_send, edge_recv,
    ) = refs
    me = lax.axis_index("row")
    peers = devices // 4
    core, side, place = lax.rem(me, 2), lax.rem(lax.div(me, 2), 2), lax.div(me, 4)
    partner, mate = me + 1 - 2 * core, me + 2 - 4 * side
    piece = sums.shape[1] // devices
    extent = grad.shape[3]
    reach = above.shape[3]
    has_before, has_after = me > 0, me < devices - 1

    def rows_of(core_at, side_at, index):
        start = ((core_at * 2 + side_at) * peers + index) * piece
        return pl.ds(pl.multiple_of(start, piece), piece)

    def to_pair(side_at, index, core_at):
        return send(
            sums.at[:, rows_of(core_at, side_at, index)], from_pair.at[side_at, index],
            pair_send.at[side_at, index], pair_recv.at[side_at, index], partner,
        )

    def to_side(index):
        return send(
            to_mate.at[index], from_mate.at[index], mate_send.at[index], mate_recv.at[index], mate
        )

    def to_place(index, slot):
        return send(
            to_peer.at[index], from_peer.at[slot],
            peer_send.at[index], peer_recv.at[slot], 4 * index + 2 * side + core,
        )

    def spread(index, slot):
        part = renewed.at[:, rows_of(core, side, slot)]
        return send(
            part, part, spread_send.at[index], spread_recv.at[slot], 4 * index + 2 * side + core
        )

    def cross(side_at, index):
        part = renewed.at[:, rows_of(core, side_at, index)]
        return send(part, part, cross_send.at[index], cross_recv.at[index], mate)

    def back(core_at, side_at, index):
        part = renewed.at[:, rows_of(core_at, side_at, index)]
        return send(
            part, part, back_send.at[side_at, index], back_recv.at[side_at, index], partner
        )

    def after_me(step):
        return lax.rem(place + 1 + step, peers)

    def before_me(step):
        return lax.rem(place + peers - 1 - step, peers)

    other = me - 1 + 2 * core
    beside = (other >= 0) & (other < devices)
    barrier = pltpu.get_barrier_semaphore()

    def signal(device):
        pl.semaphore_signal(barrier, inc=1, device_id={"row": device}, device_id_type=MESH)

    signal(partner)
    signal(mate)

    @pl.loop(0, peers - 1)
    def _(step):
        signal(4 * after_me(step) + 2 * side + core)

    @pl.when(beside)
    def _():
        signal(other)

    pl.semaphore_wait(barrier, peers + 1 + beside.astype(jnp.int32))

    pair_loss = send(loss, loss_of.at[0], loss_send.at[0], loss_recv.at[0], partner)
    mate_loss = send(loss_of.at[1], loss_of.at[2], loss_send.at[1], loss_recv.at[1], mate)
    pair_loss.start()

    @pl.loop(0, peers)
    def _(step):
        to_pair(1 - side, after_me(step), 1 - core).start()

    @pl.loop(0, peers)
    def _(step):
        to_pair(side, after_me(step), 1 - core).start()

    up = send(
        grad.at[:, :, :, pl.ds(0, reach)], below, edge_send.at[0], edge_recv.at[0], me - 1
    )
    down = send(
        grad.at[:, :, :, pl.ds(extent - reach, reach)], above,
        edge_send.at[1], edge_recv.at[1], me + 1,
    )

    pair_loss.wait()
    loss_of[1] = loss[...] + loss_of[0]
    mate_loss.start()

    def add_pair(side_at, index):
        to_pair(side_at, index, core).wait_recv()
        return sums[:, rows_of(core, side_at, index), :] + from_pair[side_at, index]

    @pl.loop(0, peers)
    def _(step):
        index = after_me(step)
        to_mate[index] = add_pair(1 - side, index)
        to_side(index).start()

    pl.when(has_before)(up.start)
    pl.when(has_after)(down.start)

    mate_loss.wait()
    quad_loss = loss_of[1] + loss_of[2]

    def fill(target, slot, index):
        both = add_pair(side, index)
        to_side(index).wait_recv()
        both = both + from_mate[index]
        for plane in range(3):
            target[slot, plane * piece : (plane + 1) * piece] = both[plane]
        target[slot, 3 * piece :] = quad_loss

    @pl.loop(0, peers - 1)
    def _(step):
        index = after_me(step)
        fill(to_peer, index, index)
        to_place(index, place).start()

    fill(from_peer, place, place)

    rate = object_rate(probe)

    @pl.loop(0, peers - 1)
    def _(step):
        index = before_me(step)
        to_place(index, index).wait_recv()

    total = from_peer[0]
    for index in range(1, peers):
        total = total + from_peer[index]
    loss_out[...] = total[3 * piece :]
    mine = rows_of(core, side, place)
    weight = total[2 * piece : 3 * piece] + DAMPING
    for part in range(2):
        step = PROBE_RATE * total[part * piece : (part + 1) * piece] / weight
        renewed[part, mine, :] = probe[part, mine, :] - step

    @pl.loop(0, peers - 1)
    def _(step):
        spread(after_me(step), place).start()

    cross(side, place).start()
    back(core, side, place).start()

    if not last:
        for plane in planes_of(grad):
            rows = (*plane, slice(reach, extent - reach))
            field_out[rows] = field[rows] - rate * grad[rows]

    @pl.loop(0, peers - 1)
    def _(step):
        index = before_me(step)
        spread(index, index).wait_recv()
        cross(side, index).start()
        back(core, side, index).start()

    @pl.loop(0, peers)
    def _(step):
        index = lax.rem(place + peers - step, peers)
        cross(1 - side, index).wait_recv()
        back(core, 1 - side, index).start()

    @pl.when(has_before)
    def _():
        down.wait_recv()

    @pl.when(me == 0)
    def _():
        above[...] = jnp.zeros_like(above)

    if last:
        above_out[...] = above[...]
    else:
        for plane in planes_of(grad):
            rows = (*plane, slice(0, reach))
            field_out[rows] = field[rows] - rate * (grad[rows] + above[plane])

    @pl.when(has_after)
    def _():
        up.wait_recv()

    @pl.when(me == devices - 1)
    def _():
        below[...] = jnp.zeros_like(below)

    if last:
        below_out[...] = below[...]
    else:
        for plane in planes_of(grad):
            rows = (*plane, slice(extent - reach, extent))
            field_out[rows] = field[rows] - rate * (grad[rows] + below[plane])
        empty = (*field.shape[:3], MARGIN, LANES)

        @pl.when(me == 0)
        def _():
            field_out[:, :, :, :MARGIN] = jnp.zeros(empty, jnp.float32)

        @pl.when(me == devices - 1)
        def _():
            field_out[:, :, :, extent - MARGIN :] = jnp.zeros(empty, jnp.float32)

    for side_at in range(2):

        @pl.loop(0, peers)
        def _(index, side_at=side_at):
            back(1 - core, side_at, index).wait_recv()

    probe_out[...] = renewed[...]

    for side_at in range(2):

        @pl.loop(0, peers)
        def _(index, side_at=side_at):
            to_pair(side_at, index, 1 - core).wait_send()
            back(core, side_at, index).wait_send()

    @pl.loop(0, peers)
    def _(index):
        to_side(index).wait_send()
        cross(side, index).wait_send()

    @pl.loop(0, peers - 1)
    def _(step):
        index = after_me(step)
        to_place(index, place).wait_send()
        spread(index, place).wait_send()

    pl.when(has_before)(up.wait_send)
    pl.when(has_after)(down.wait_send)


def renew(grad, sums, loss, field, probe, last):
    devices = lax.axis_size("row")
    peers = devices // 4
    piece = sums.shape[1] // devices
    reach = MARGIN if last else 2 * MARGIN
    vmem = pl.BlockSpec(memory_space=pltpu.VMEM)
    edge_shape = (*field.shape[:3], reach, LANES)
    edge = pltpu.VMEM(edge_shape, jnp.float32)
    edge_out = jax.ShapeDtypeStruct(edge_shape, jnp.float32)
    packet = pltpu.VMEM((peers, 3 * piece + 8, LANES), jnp.float32)
    part = pltpu.VMEM((peers, 3, piece, LANES), jnp.float32)
    each = pltpu.SemaphoreType.DMA((peers,))
    double = pltpu.SemaphoreType.DMA((2, peers))
    two = pltpu.SemaphoreType.DMA((2,))
    objects = (edge_out, edge_out) if last else (jax.ShapeDtypeStruct(field.shape, jnp.float32),)
    outs = objects + (
        jax.ShapeDtypeStruct(probe.shape, jnp.float32),
        jax.ShapeDtypeStruct(loss.shape, jnp.float32),
    )
    operands = (grad, sums, loss, probe) + (() if last else (field,))
    return pl.pallas_call(
        functools.partial(renew_kernel, devices, last),
        out_shape=outs,
        in_specs=[vmem] * len(operands),
        out_specs=(vmem,) * len(outs),
        scratch_shapes=[
            pltpu.VMEM((2, peers, 3, piece, LANES), jnp.float32),
            pltpu.VMEM((3, *loss.shape), jnp.float32),
            part,
            part,
            packet,
            packet,
            pltpu.VMEM(probe.shape, jnp.float32),
            edge,
            edge,
            two, two, double, double, each, each, each, each,
            each, each, each, each, double, double,
            two, two,
        ],
        compiler_params=pltpu.CompilerParams(
            collective_id=2 if last else 1, has_side_effects=True, vmem_limit_bytes=VMEM_LIMIT
        ),
    )(*operands)


def finish_kernel(
    count, field, grad, above, below, old, probe, *refs
):
    *losses, field_out, probe_out, misfit_out = refs
    rate = object_rate(old)
    length = probe_out.shape[1]
    tile = field_out.shape[2]
    for plane in planes_of(field):
        which, part, index = plane
        columns = slice(index * LANES, (index + 1) * LANES)
        for start, stop, extra in (
            (0, MARGIN, above), (MARGIN, tile - MARGIN, None), (tile - MARGIN, tile, below)
        ):
            rows = (*plane, slice(MARGIN + start, MARGIN + stop))
            value = grad[rows] if extra is None else grad[rows] + extra[plane]
            field_out[which, part, start:stop, columns] = field[rows] - rate * value
    for part in range(length // LANES):
        columns = slice(part * LANES, (part + 1) * LANES)
        probe_out[:, :, columns] = probe[:, part * length : (part + 1) * length]
    for index, loss in enumerate(losses):
        misfit_out[index] = jnp.sum(loss[...]) / count


def finish(count, field, grad, above, below, old, probe, losses, shapes):
    vmem = pl.BlockSpec(memory_space=pltpu.VMEM)
    return pl.pallas_call(
        functools.partial(finish_kernel, count),
        out_shape=tuple(
            jax.ShapeDtypeStruct(shape, jnp.float32) for shape in (*shapes, (len(losses),))
        ),
        in_specs=[vmem] * (6 + len(losses)),
        out_specs=(vmem, vmem, pl.BlockSpec(memory_space=pltpu.SMEM)),
        compiler_params=pltpu.CompilerParams(vmem_limit_bytes=VMEM_LIMIT),
    )(field, grad, above, below, old, probe, *losses)


def shards(object_field, probe, intensity, row_offset, col_offset, slice_first):
    length = probe.shape[1]
    count = float(intensity.shape[0] * lax.axis_size("row") * length * length)
    field, light = first_field(object_field, probe)
    losses = []
    for step in range(ITERS):
        grad, sums, loss = local_terms(
            field, light, intensity, row_offset, col_offset, slice_first
        )
        old = light
        if step < ITERS - 1:
            field, light, loss = renew(grad, sums, loss, field, light, False)
        else:
            above, below, light, loss = renew(grad, sums, loss, field, light, True)
        losses.append(loss)
    shapes = (object_field.shape, probe.shape)
    return finish(count, field, grad, above, below, old, light, losses, shapes)


def solution(mesh):
    placed = (
        P("scan", None, "row", None),
        P("scan", None, None),
        P(("scan", "row"), None, None),
        P(("scan", "row")),
        P(("scan", "row")),
        P(("scan", "row")),
    )
    return jax.shard_map(
        shards,
        mesh=mesh,
        in_specs=placed,
        out_specs=(P("scan", None, "row", None), P("scan", None, None), P("scan")),
        check_vma=False,
    )
```
